128 devices in a mesh: zone: 2 (over core), dom: 64 (over y, z, x).
Axes of the slice: x: 4, y: 4, z: 4, core: 2. Of those that a mesh axis runs over, the one named last changes fastest.
Arguments:
- adjoint_start: float32 [2, 32, 196608], P('zone', None, 'dom'), may hold values from -6 to 6
- right_side: float32 [2, 32, 196608], P('zone', None, 'dom'), may hold values from -6 to 6
- send_rows: int32 [2, 64, 64, 24], P('zone', 'dom'), may hold values from 0 to 3071, as said below
- send_count: int32 [2, 64, 64], P('zone', 'dom'), may hold values from 0 to 24, as said below
- face_left: int32 [98304], P('dom'), may hold values from 0 to 511
- face_right: int32 [98304], P('dom'), may hold values from 0 to 768, as said below
- block_left: bfloat16 [6, 6, 98304], P(None, None, 'dom'), may hold values from -1.75 to 1.75
- block_right: bfloat16 [6, 6, 98304], P(None, None, 'dom'), may hold values from -1.75 to 1.75
- cell_diag: bfloat16 [6, 6, 32768], P(None, None, 'dom'), may hold values from -1.61 to 6.65
- cell_prec: bfloat16 [6, 6, 32768], P(None, None, 'dom'), may hold values from -0.162 to 0.49
- elem_nodes: int32 [27, 24576], P(None, 'dom'), may hold values from 0 to 4607, as said below
- elem_mat: bfloat16 [27, 27, 24576], P(None, None, 'dom'), may hold values from -0.65 to 2
- elem_count: int32 [64], P('dom'), may hold values from 192 to 384, as said below
- node_scale: float32 [196608], P('dom'), may hold values from 0.1 to 0.3
- iface_cell: int32 [16384], P('dom'), may hold values from 0 to 511
- iface_slot: int32 [4, 16384], P(None, 'dom'), may hold values from 0 to 2047, as said below
- iface_weight: float32 [4, 16384], P(None, 'dom'), may hold values from 0.05 to 0.45
- flux_in: float32 [6, 16384], P(None, 'dom'), may hold values from -6 to 6
- flux_out: float32 [6, 16384], P(None, 'dom'), may hold values from -3 to 3
- iface_count: int32 [64], P('dom'), may hold values from 64 to 256, as said below
- iface_nodes: int32 [64, 64, 32], P('dom'), may hold values from 0 to 3071
- iface_pairs: int32 [64, 64], P('dom'), may hold values from 0 to 32, as said below
Outputs:
- adjoint: float32 [2, 32, 196608], P('zone', None, 'dom')
- residual: float32 [2, 32, 196608], P('zone', None, 'dom')
The draws below stay inside these ranges and needn't reach their ends.
Inputs may be any that keep to these rules, and one draw needn't show every extreme that they name: `send_rows`: slots at or beyond a list's count carry no data. In zone 0 every group of 6 slots 6j to 6j + 5 lists the rows v * 512 + c, v = 0 to 5, of one cell c. `send_count`: counts of zone 0 are multiples of 6; a subdomain sends nothing to itself; some list of each zone is full. `face_right`: below 512 the subdomain's own cells; 512 + p * 4 + j the ghost cell j from subdomain p, always with 6 j below that list's count; 768 the wall. `elem_nodes`: below 3072 the subdomain's own rows; 3072 + p * 24 + g the ghost slot g from subdomain p, always with g below that list's count. `elem_count`: live elements are the first ones of a subdomain; some subdomain has 384. `iface_slot`: p * 32 + k names slot k of solid subdomain p's list for this fluid subdomain, always with k below that list's count. `iface_count`: live faces are the first ones of a subdomain; some subdomain has 256. `iface_pairs`: rows are solid subdomain s, columns fluid subdomain f; the pair s = f has 16 or more; some list is full.
All inputs are finite; a program needn't handle non-finite values.
Results may differ from the reference program's by a relative error of at most 0.0003.
Values sent between devices are 32-bit elements; how exact they have to be, the bound alone decides.
A program may use at most 128 MiB of HBM per device.

```python
import math
import jax
import jax.numpy as jnp
from jax import lax

COLS = 32
NV = 6
NODES_EL = 27
CELLS = 512
SWEEPS = 2
ROWS = 3072
FACES = 1536
ELEMS = 384
GHOST = 24
SLOTS = 32
IFACES = 256
SUBDOMAINS = 64


def cycle_offsets(peer_count):
    sender = jnp.arange(peer_count)[:, None]
    target = jnp.arange(peer_count)[None, :]
    return (target - sender) % peer_count


def ghost_counts(key):
    peer_count = SUBDOMAINS
    offset = cycle_offsets(peer_count)
    nearby = (offset == 1) | (offset == peer_count - 1) | (offset == 2) | (offset == peer_count - 2) | (offset == peer_count // 2)
    result = []
    for zone_no in range(2):
        zone_key = jax.random.fold_in(jax.random.fold_in(key, 9103), zone_no)
        k_extra, k_count, k_full = jax.random.split(zone_key, 3)
        extras = jax.random.randint(k_extra, (peer_count, peer_count), 0, 8) < 6
        linked = (nearby | extras) & (offset != 0)
        if zone_no == 0:
            amount = NV * jax.random.randint(k_count, (peer_count, peer_count), GHOST // 12, GHOST // NV + 1)
        else:
            amount = jax.random.randint(k_count, (peer_count, peer_count), GHOST // 2, GHOST + 1)
        chosen = jax.random.randint(k_full, (), 0, peer_count)
        forced = (jnp.arange(peer_count)[:, None] == chosen) & (offset == 1)
        amount = jnp.where(forced, GHOST, amount)
        result.append(jnp.where(linked | forced, amount, 0))
    return jnp.stack(result).astype(jnp.int32)


def iface_counts(key):
    peer_count = SUBDOMAINS
    offset = cycle_offsets(peer_count)
    nearby = (offset == 0) | (offset == 1) | (offset == peer_count - 1) | (offset == peer_count // 2)
    k_extra, k_count, k_full = jax.random.split(jax.random.fold_in(key, 9521), 3)
    extras = jax.random.randint(k_extra, (peer_count, peer_count), 0, 8) < 6
    amount = jax.random.randint(k_count, (peer_count, peer_count), SLOTS // 2, SLOTS + 1)
    chosen = jax.random.randint(k_full, (), 0, peer_count)
    forced = (jnp.arange(peer_count)[:, None] == chosen) & (offset == 0)
    amount = jnp.where(forced, SLOTS, amount)
    return jnp.where(nearby | extras, amount, 0).astype(jnp.int32)


def draw_send_count(key, part):
    return ghost_counts(key)


def draw_send_rows(key, part):
    peer_count = SUBDOMAINS
    k_cell, k_node = jax.random.split(jax.random.fold_in(key, 9217))
    cell_pick = jax.random.randint(k_cell, (peer_count, peer_count, GHOST // NV), 0, CELLS)
    fluid_rows = (cell_pick[:, :, :, None] + CELLS * jnp.arange(NV)[None, None, None, :]).reshape(peer_count, peer_count, GHOST)
    solid_rows = jax.random.randint(k_node, (peer_count, peer_count, GHOST), 0, ROWS)
    return jnp.stack([fluid_rows, solid_rows]).astype(jnp.int32)


def draw_face_right(key, part):
    peer_count = SUBDOMAINS
    counts = ghost_counts(key)[0]
    ghost_cells = GHOST // NV
    sub_keys = jax.random.split(jax.random.fold_in(key, 9311), 4)
    face_kind = jax.random.randint(sub_keys[0], (peer_count, FACES), 0, 16)
    source = jax.random.randint(sub_keys[1], (peer_count, FACES), 0, peer_count)
    slot_pick = jax.random.randint(sub_keys[2], (peer_count, FACES), 0, ghost_cells)
    own_cell = jax.random.randint(sub_keys[3], (peer_count, FACES), 0, CELLS)
    receiver = jnp.arange(peer_count)[:, None]
    available = counts[source, receiver]
    usable = (face_kind < 8) & (NV * slot_pick < available)
    remote = CELLS + source * ghost_cells + slot_pick
    wall_cell = CELLS + peer_count * ghost_cells
    chosen = jnp.where(usable, remote, jnp.where(face_kind == 15, wall_cell, own_cell))
    return chosen.reshape(-1).astype(jnp.int32)


def draw_elem_nodes(key, part):
    peer_count = SUBDOMAINS
    counts = ghost_counts(key)[1]
    sub_keys = jax.random.split(jax.random.fold_in(key, 9337), 4)
    out_shape = (NODES_EL, peer_count, ELEMS)
    face_kind = jax.random.randint(sub_keys[0], out_shape, 0, 2)
    source = jax.random.randint(sub_keys[1], out_shape, 0, peer_count)
    slot_pick = jax.random.randint(sub_keys[2], out_shape, 0, GHOST)
    own_node = jax.random.randint(sub_keys[3], out_shape, 0, ROWS)
    receiver = jnp.arange(peer_count)[None, :, None]
    available = counts[source, receiver]
    usable = (face_kind == 0) & (slot_pick < available)
    chosen = jnp.where(usable, ROWS + source * GHOST + slot_pick, own_node)
    return chosen.reshape(NODES_EL, peer_count * ELEMS).astype(jnp.int32)


def draw_elem_count(key, part):
    peer_count = SUBDOMAINS
    k_count, k_full = jax.random.split(jax.random.fold_in(key, 9419))
    amount = ELEMS - jax.random.randint(k_count, (peer_count,), 0, ELEMS // 2 + 1)
    chosen = jax.random.randint(k_full, (), 0, peer_count)
    return jnp.where(jnp.arange(peer_count) == chosen, ELEMS, amount).astype(jnp.int32)


def draw_iface_pairs(key, part):
    return iface_counts(key)


def draw_iface_slot(key, part):
    peer_count = SUBDOMAINS
    counts = iface_counts(key)
    sub_keys = jax.random.split(jax.random.fold_in(key, 9631), 2)
    shifts = jnp.array([0, 1, peer_count - 1, peer_count // 2], jnp.int32)
    kind = jax.random.randint(sub_keys[0], (4, peer_count, IFACES), 0, 4)
    slot_pick = jax.random.randint(sub_keys[1], (4, peer_count, IFACES), 0, SLOTS)
    node_no = jnp.arange(4)[:, None, None]
    face_no = jnp.arange(IFACES)[None, None, :]
    first_face = face_no == 0
    kind = jnp.where(first_face & (node_no == 0), 2, jnp.where(first_face & (node_no == 1), 1, kind))
    slot_pick = jnp.where(first_face & (node_no < 2), 0, slot_pick)
    receiver = jnp.arange(peer_count)[None, :, None]
    source = (receiver + shifts[kind]) % peer_count
    available = counts[source, receiver]
    own_count = counts[receiver, receiver]
    usable = slot_pick < available
    chosen = jnp.where(usable, source * SLOTS + slot_pick, receiver * SLOTS + slot_pick % own_count)
    return chosen.reshape(4, peer_count * IFACES).astype(jnp.int32)


def draw_iface_count(key, part):
    peer_count = SUBDOMAINS
    k_level, k_full = jax.random.split(jax.random.fold_in(key, 9743))
    levels = jnp.array([IFACES, IFACES // 2, IFACES // 4], jnp.int32)
    amount = levels[jax.random.randint(k_level, (peer_count,), 0, 3)]
    chosen = jax.random.randint(k_full, (), 0, peer_count)
    return jnp.where(jnp.arange(peer_count) == chosen, IFACES, amount).astype(jnp.int32)


def dominant(key, size, count, low, high, deviation):
    k_mid, k_off = jax.random.split(key)
    identity = jnp.eye(size, dtype=jnp.float32)[:, :, None]
    middle = jax.random.uniform(k_mid, (1, 1, count), jnp.float32, low, high)
    spread = deviation * jnp.clip(jax.random.normal(k_off, (size, size, count), jnp.float32), -4.0, 4.0)
    return identity * middle + spread


def draw_cell_diag(key, part):
    return dominant(jax.random.fold_in(key, 9851), NV, CELLS * SUBDOMAINS, 3.0, 5.0, 0.4).astype(jnp.bfloat16)


def draw_cell_prec(key, part):
    return dominant(jax.random.fold_in(key, 9859), NV, CELLS * SUBDOMAINS, 0.15, 0.3, 0.04).astype(jnp.bfloat16)


def draw_elem_mat(key, part):
    return dominant(jax.random.fold_in(key, 9871), NODES_EL, ELEMS * SUBDOMAINS, 0.8, 1.2, 0.15).astype(jnp.bfloat16)


def plant(values, own_key, smallest, largest):
    spot = [jax.random.randint(jax.random.fold_in(own_key, axis), (), 0, length) for axis, length in enumerate(values.shape)]
    widest = values.shape.index(max(values.shape))
    next_to = spot[:widest] + [(spot[widest] + 1) % values.shape[widest]] + spot[widest + 1:]
    return values.at[tuple(spot)].set(smallest).at[tuple(next_to)].set(largest)


def level_of(stream_key, shape, cuts, least, high):
    def one(dim, shards_of):
        heights = jax.random.uniform(jax.random.fold_in(jax.random.fold_in(stream_key, 6), dim), (shards_of,), jnp.float32, least / len(cuts), high / len(cuts))
        return jnp.repeat(jnp.exp(heights), shape[dim] // shards_of).reshape((-1,) + (1,) * (len(shape) - dim - 1))

    level = one(*cuts[0])
    for cut in cuts[1:]:
        level = level * one(*cut)
    return level


def scatter_about(stream_key, shape, width, reach, cuts=(), kind=jnp.bfloat16):
    factor_of = level_of(stream_key, shape, cuts, -0.22, 0.18) if cuts else 1.0
    values = jax.random.normal(stream_key, shape, jnp.float32) * width * factor_of
    return jnp.minimum(jnp.maximum(values, -reach), reach).astype(kind)


def setup_inputs(seed: int = 0) -> dict:
    key_of = jax.random.split(jax.random.key(seed), 23)
    adjoint_start = scatter_about(key_of[0], (2, COLS, ROWS * SUBDOMAINS), 1.0, 6.0, ((0, 2), (2, 64)), jnp.float32)
    right_side = scatter_about(key_of[1], (2, COLS, ROWS * SUBDOMAINS), 1.0, 6.0, ((0, 2), (2, 64)), jnp.float32)
    send_rows = draw_send_rows(jax.random.fold_in(key_of[22], 71), 0)
    send_count = draw_send_count(jax.random.fold_in(key_of[22], 71), 0)
    face_left = plant(jax.random.randint(key_of[4], (FACES * SUBDOMAINS,), 0, CELLS), jax.random.fold_in(key_of[4], 1), 0, CELLS - 1).astype(jnp.int32)
    face_right = draw_face_right(jax.random.fold_in(key_of[22], 71), 0)
    block_left = scatter_about(key_of[6], (NV, NV, FACES * SUBDOMAINS), (2 * NV) ** -0.5, 1.75, ((2, 64),))
    block_right = scatter_about(key_of[7], (NV, NV, FACES * SUBDOMAINS), (2 * NV) ** -0.5, 1.75, ((2, 64),))
    cell_diag = draw_cell_diag(jax.random.fold_in(key_of[22], 71), 0)
    cell_prec = draw_cell_prec(jax.random.fold_in(key_of[22], 71), 0)
    elem_nodes = draw_elem_nodes(jax.random.fold_in(key_of[22], 71), 0)
    elem_mat = draw_elem_mat(jax.random.fold_in(key_of[22], 71), 0)
    elem_count = draw_elem_count(jax.random.fold_in(key_of[22], 71), 0)
    node_scale = jnp.clip(jnp.exp(math.log(0.3) - 1.0986123 * jax.random.uniform(key_of[13], (ROWS * SUBDOMAINS,), jnp.float32) ** level_of(key_of[13], (ROWS * SUBDOMAINS,), ((0, 64),), -0.2, 0.2)), 0.1, 0.3)
    iface_cell = plant(jax.random.randint(key_of[14], (IFACES * SUBDOMAINS,), 0, CELLS), jax.random.fold_in(key_of[14], 1), 0, CELLS - 1).astype(jnp.int32)
    iface_slot = draw_iface_slot(jax.random.fold_in(key_of[22], 71), 0)
    iface_weight = jnp.clip(0.05 + 0.39999999 * jax.random.uniform(key_of[16], (4, IFACES * SUBDOMAINS), jnp.float32) ** level_of(key_of[16], (4, IFACES * SUBDOMAINS), ((1, 64),), -0.2, 0.2), 0.05, 0.45)
    flux_in = scatter_about(key_of[17], (NV, IFACES * SUBDOMAINS), 1.0, 6.0, ((1, 64),), jnp.float32)
    flux_out = scatter_about(key_of[18], (NV, IFACES * SUBDOMAINS), 0.5, 3.0, ((1, 64),), jnp.float32)
    iface_count = draw_iface_count(jax.random.fold_in(key_of[22], 71), 0)
    iface_nodes = plant(jax.random.randint(key_of[20], (SUBDOMAINS, SUBDOMAINS, SLOTS), 0, ROWS), jax.random.fold_in(key_of[20], 1), 0, ROWS - 1).astype(jnp.int32)
    iface_pairs = draw_iface_pairs(jax.random.fold_in(key_of[22], 71), 0)
    return {"adjoint_start": adjoint_start, "right_side": right_side, "send_rows": send_rows, "send_count": send_count, "face_left": face_left, "face_right": face_right, "block_left": block_left, "block_right": block_right, "cell_diag": cell_diag, "cell_prec": cell_prec, "elem_nodes": elem_nodes, "elem_mat": elem_mat, "elem_count": elem_count, "node_scale": node_scale, "iface_cell": iface_cell, "iface_slot": iface_slot, "iface_weight": iface_weight, "flux_in": flux_in, "flux_out": flux_out, "iface_count": iface_count, "iface_nodes": iface_nodes, "iface_pairs": iface_pairs}


PRECISE = lax.Precision.HIGHEST


def block_apply(blocks, values):
    summed = blocks[0][None, :, :] * values[:, 0:1, :]
    for position in range(1, blocks.shape[0]):
        summed = summed + blocks[position][None, :, :] * values[:, position:position + 1, :]
    return summed


def fluid_image(own, ghosts, left_ids, right_ids, blk_left, blk_right, diagonal):
    var_count = diagonal.shape[0]
    columns = own.shape[0]
    cell_count = own.shape[1] // var_count
    own_cells = own.reshape(columns, var_count, cell_count)
    ghost_cells = jnp.transpose(ghosts.reshape(columns, -1, var_count), (0, 2, 1))
    wall_cell = jnp.zeros((columns, var_count, 1), jnp.float32)
    widened = jnp.concatenate([own_cells, ghost_cells, wall_cell], axis=2)
    face_jump = jnp.take(own_cells, left_ids, axis=2) - jnp.take(widened, right_ids, axis=2)
    to_left = block_apply(blk_left.astype(jnp.float32), face_jump)
    to_right = block_apply(blk_right.astype(jnp.float32), face_jump)
    summed = jnp.zeros_like(widened).at[:, :, left_ids].add(to_left).at[:, :, right_ids].add(to_right)
    own_image = summed[:, :, :cell_count] + block_apply(diagonal.astype(jnp.float32), own_cells)
    ghost_total = ghost_cells.shape[2]
    ghost_image = jnp.transpose(summed[:, :, cell_count:cell_count + ghost_total], (0, 2, 1)).reshape(ghosts.shape)
    return own_image.reshape(columns, -1), ghost_image


def solid_image(own, ghosts, node_ids, matrices, elem_alive):
    columns, row_count = own.shape
    widened = jnp.concatenate([own, ghosts.reshape(columns, -1)], axis=1)
    flat_ids = node_ids.reshape(-1)
    picked = jnp.take(widened, flat_ids, axis=1).reshape(columns, node_ids.shape[0], node_ids.shape[1])
    pushed = jnp.einsum("jie,cje->cie", matrices.astype(jnp.float32), picked, precision=PRECISE)
    pushed = pushed * elem_alive[None, None, :]
    summed = jnp.zeros_like(widened).at[:, flat_ids].add(pushed.reshape(columns, -1))
    return summed[:, :row_count], summed[:, row_count:].reshape(ghosts.shape)


def fluid_outgoing(own, cell_ids, slot_ids, weights, flux, face_alive, peer_count, slot_count):
    columns = own.shape[0]
    own_cells = own.reshape(columns, flux.shape[0], -1)
    at_faces = jnp.take(own_cells, cell_ids, axis=2)
    strength = jnp.sum(flux[None, :, :] * at_faces, axis=1) * face_alive[None, :]
    spread_vals = weights[None, :, :] * strength[:, None, :]
    outgoing = jnp.zeros((columns, peer_count * slot_count), jnp.float32)
    outgoing = outgoing.at[:, slot_ids.reshape(-1)].add(spread_vals.reshape(columns, -1))
    return outgoing.reshape(columns, peer_count, slot_count)


def fluid_incoming(incoming, cell_ids, slot_ids, weights, flux, face_alive, cell_count):
    columns = incoming.shape[0]
    flattened = incoming.reshape(columns, -1)
    picked = jnp.take(flattened, slot_ids.reshape(-1), axis=1).reshape(columns, slot_ids.shape[0], slot_ids.shape[1])
    wall_temp = jnp.sum(weights[None, :, :] * picked, axis=1) * face_alive[None, :]
    added = flux[None, :, :] * wall_temp[:, None, :]
    coupling = jnp.zeros((columns, flux.shape[0], cell_count), jnp.float32).at[:, :, cell_ids].add(added)
    return coupling.reshape(columns, -1)


def reference(adjoint_start, right_side, send_rows, send_count, face_left, face_right, block_left, block_right, cell_diag, cell_prec, elem_nodes, elem_mat, elem_count, node_scale, iface_cell, iface_slot, iface_weight, flux_in, flux_out, iface_count, iface_nodes, iface_pairs):
    peer_count = SUBDOMAINS
    peer_ids = jnp.arange(peer_count)
    adjoint = adjoint_start.reshape(2, COLS, peer_count, ROWS)
    forcing = right_side.reshape(2, COLS, peer_count, ROWS)
    slot_live = (jnp.arange(GHOST)[None, None, None, :] < send_count[:, :, :, None]).astype(jnp.float32)
    pair_live = (jnp.arange(SLOTS)[None, None, :] < iface_pairs[:, :, None]).astype(jnp.float32)
    face_live = (jnp.arange(IFACES)[None, :] < iface_count[:, None]).astype(jnp.float32)
    elem_live = (jnp.arange(ELEMS)[None, :] < elem_count[:, None]).astype(jnp.float32)
    left_all = face_left.reshape(peer_count, FACES)
    right_all = face_right.reshape(peer_count, FACES)
    bleft_all = block_left.reshape(NV, NV, peer_count, FACES)
    bright_all = block_right.reshape(NV, NV, peer_count, FACES)
    diag_all = cell_diag.reshape(NV, NV, peer_count, CELLS)
    nodes_all = elem_nodes.reshape(NODES_EL, peer_count, ELEMS)
    mats_all = elem_mat.reshape(NODES_EL, NODES_EL, peer_count, ELEMS)
    cell_all = iface_cell.reshape(peer_count, IFACES)
    slot_all = iface_slot.reshape(4, peer_count, IFACES)
    weight_all = iface_weight.reshape(4, peer_count, IFACES)
    fin_all = flux_in.reshape(NV, peer_count, IFACES)
    fout_all = flux_out.reshape(NV, peer_count, IFACES)

    def to_fluid(fluid_no):
        incoming = adjoint[1][:, peer_ids[:, None], iface_nodes[:, fluid_no, :]] * pair_live[None, :, fluid_no, :]
        return fluid_incoming(incoming, cell_all[fluid_no], slot_all[:, fluid_no], weight_all[:, fluid_no], fin_all[:, fluid_no], face_live[fluid_no], CELLS)

    coupling_fluid = jnp.moveaxis(lax.map(to_fluid, peer_ids), 0, 1)

    def from_fluid(carry, fluid_no):
        outgoing = fluid_outgoing(adjoint[0][:, fluid_no], cell_all[fluid_no], slot_all[:, fluid_no], weight_all[:, fluid_no], fout_all[:, fluid_no], face_live[fluid_no], peer_count, SLOTS)
        carry = carry.at[:, peer_ids[:, None], iface_nodes[:, fluid_no, :]].add(outgoing * pair_live[None, :, fluid_no, :])
        return carry, None

    coupling_solid = lax.scan(from_fluid, jnp.zeros((COLS, peer_count, ROWS), jnp.float32), peer_ids)[0]
    coupling = jnp.stack([coupling_fluid, coupling_solid])

    residual = jnp.zeros_like(adjoint)
    for sweep_no in range(SWEEPS):
        images = []
        for zone_no in range(2):
            current = adjoint[zone_no]

            def visit(carry, dom_no, zone_no=zone_no, current=current):
                rows_in = send_rows[zone_no][:, dom_no, :]
                live_in = slot_live[zone_no][:, dom_no, :][None]
                ghosts = current[:, peer_ids[:, None], rows_in] * live_in
                own = current[:, dom_no]
                if zone_no == 0:
                    own_image, ghost_image = fluid_image(own, ghosts, left_all[dom_no], right_all[dom_no], bleft_all[:, :, dom_no], bright_all[:, :, dom_no], diag_all[:, :, dom_no])
                else:
                    own_image, ghost_image = solid_image(own, ghosts, nodes_all[:, dom_no], mats_all[:, :, dom_no], elem_live[dom_no])
                carry = carry.at[:, dom_no].add(own_image)
                carry = carry.at[:, peer_ids[:, None], rows_in].add(ghost_image * live_in)
                return carry, None

            images.append(lax.scan(visit, jnp.zeros((COLS, peer_count, ROWS), jnp.float32), peer_ids)[0])
        image = jnp.stack(images)
        residual = forcing - coupling - image
        fluid_res = jnp.moveaxis(residual[0].reshape(COLS, peer_count, NV, CELLS), 2, 1).reshape(COLS, NV, peer_count * CELLS)
        fluid_step = block_apply(cell_prec.astype(jnp.float32), fluid_res)
        fluid_step = jnp.moveaxis(fluid_step.reshape(COLS, NV, peer_count, CELLS), 1, 2).reshape(COLS, peer_count, ROWS)
        solid_step = node_scale.reshape(peer_count, ROWS)[None, :, :] * residual[1]
        adjoint = adjoint + jnp.stack([fluid_step, solid_step])
    return adjoint.reshape(2, COLS, peer_count * ROWS), residual.reshape(2, COLS, peer_count * ROWS)
```

```python
import jax
import jax.numpy as jnp
from jax import lax
from jax.experimental import pallas as pl
from jax.experimental.pallas import tpu as pltpu
from jax.sharding import PartitionSpec as P

MESH = pl.DeviceIdType.MESH
F32 = jnp.float32
BF16 = jnp.bfloat16
I32 = jnp.int32
EXACT = lax.Precision.HIGHEST

SWEEPS = 2
COLS = 32
NV = 6
CELLS = 512
ROWS = 3072
FACES = 1536
ELEMS = 384
NODES = 27
GHOST = 24
SLOTS = 32
IFACES = 256
PEERS = 64
LANES = PEERS * 8
EXTRA = 3 * LANES
ELEM_LANES = 28 * ELEMS
BASE = 256


def iota(shape, dim):
    return lax.broadcasted_iota(I32, shape, dim)


def dot(a, b):
    return jnp.dot(a, b, preferred_element_type=F32)


def dot_t(a, b):
    return lax.dot_general(a, b, (((1,), (1,)), ((), ())), preferred_element_type=F32)


def dot_exact(a, b):
    return jnp.dot(a, b, precision=EXACT, preferred_element_type=F32)


def split(x):
    hi = x.astype(BF16)
    lo = (x - hi.astype(F32)).astype(BF16)
    return hi, lo


def onehot(ids, count):
    return jnp.where(iota((count, ids.shape[1]), 0) == ids, 1.0, 0.0).astype(BF16)


def eight(row):
    return jnp.broadcast_to(row, (8, row.shape[1]))


def to_int(x):
    return (x + 0.5).astype(I32)


def pick_mask():
    return jnp.where(iota((PEERS, LANES), 0) == (iota((PEERS, LANES), 1) >> 3), 1.0, 0.0)


def spread_ids(table, lane_slot, mask):
    width = table.shape[1]
    chooser = jnp.where(iota((width, LANES), 0) == lane_slot, 1.0, 0.0)
    return to_int(jnp.sum(dot_exact(table, chooser) * mask, axis=0, keepdims=True))


def chunked(total, step, body):
    def run(k, carry):
        body(pl.multiple_of(k * step, 128))
        return carry

    lax.fori_loop(0, total // step, run, 0)


def wide_gather(xh, xl, blocks, hot, tags, total, step, put):
    def body(off):
        lanes = pl.ds(off, step)
        onto = hot[:, lanes]
        found = dot(xh[0 : blocks * COLS, :], onto) + dot(xl[0 : blocks * COLS, :], onto)
        tag = tags[:, lanes]
        parts = []
        for g in range(COLS // 8):
            part = jnp.zeros((8, step), F32)
            for a in range(blocks):
                r = a * COLS + g * 8
                part = jnp.where(tag == a, found[r : r + 8, :], part)
            parts.append(part)
        put(off, jnp.concatenate(parts, axis=0))

    chunked(total, step, body)


def wide_scatter(fetch, blocks, hot, tags, total, step, acc):
    acc[0 : blocks * COLS, :] = jnp.zeros((blocks * COLS, BASE), F32)

    def body(off):
        lanes = pl.ds(off, step)
        hi, lo = fetch(off)
        onto = hot[:, lanes]
        tag = tags[:, lanes]
        his, los = [], []
        for a in range(blocks):
            m8 = jnp.where(tag == a, 1.0, 0.0)
            m = jnp.concatenate([m8, m8, m8, m8], axis=0).astype(BF16)
            his.append(hi * m)
            los.append(lo * m)
        sum_hi = dot_t(jnp.concatenate(his, axis=0), onto)
        sum_lo = dot_t(jnp.concatenate(los, axis=0), onto)
        acc[0 : blocks * COLS, :] += sum_hi + sum_lo

    chunked(total, step, body)


def put_blocks(xh, xl, first, blocks):
    for k, block in enumerate(blocks):
        rows = slice((first + k) * COLS, (first + k + 1) * COLS)
        hi, lo = split(block)
        xh[rows, :] = hi
        xl[rows, :] = lo


def to_tiles(stacked):
    height = stacked.shape[0]
    if height < 128:
        stacked = jnp.concatenate([stacked, jnp.zeros((128 - height, LANES), F32)], axis=0)
    return stacked.T.reshape(PEERS, 8, 128)


def from_tiles(tiles):
    return tiles.reshape(LANES, 128).T


def kernel(
    adjoint_start,
    right_side,
    send_rows,
    send_count,
    face_left,
    face_right,
    block_left,
    block_right,
    cell_diag,
    cell_prec,
    elem_nodes,
    elem_mat,
    elem_count,
    node_scale,
    iface_cell,
    iface_slot,
    iface_weight,
    flux_in,
    flux_out,
    iface_count,
    iface_nodes,
    iface_pairs,
    out_x,
    out_r,
    ghost_tx,
    ghost_rx,
    back_tx,
    back_rx,
    pair_tx,
    pair_rx,
    fx,
    f_coupling,
    f_image,
    f_jump,
    f_right,
    f_both,
    f_diff,
    f_left,
    f_send,
    f_cell,
    f_slot,
    f_slot_tag,
    sx,
    s_coupling,
    s_mat,
    s_nodes,
    s_send,
    s_send_tag,
    s_pair,
    s_pair_tag,
    s_elem,
    s_elem_tag,
    s_picked,
    s_hi,
    s_lo,
    s_wide,
    xh,
    xl,
    acc,
    ghost_send_sem,
    ghost_recv_sem,
    back_send_sem,
    back_recv_sem,
    pair_send_sem,
    pair_recv_sem,
):
    zone = lax.axis_index("zone")
    me = lax.axis_index("dom")
    other = 1 - zone
    is_fluid = zone == 0
    is_solid = zone == 1

    barrier = pltpu.get_barrier_semaphore()

    def greet(i, carry):
        peer = lax.rem(me + i, PEERS)
        pl.semaphore_signal(barrier, inc=1, device_id=(zone, peer), device_id_type=MESH)
        return carry

    def greet_other(i, carry):
        peer = lax.rem(me + i, PEERS)
        pl.semaphore_signal(barrier, inc=1, device_id=(other, peer), device_id_type=MESH)
        return carry

    lax.fori_loop(1, PEERS, greet, 0)
    lax.fori_loop(0, PEERS, greet_other, 0)

    def copy_to(src, dst, peer, to_zone, send_sem, recv_sem):
        return pltpu.make_async_remote_copy(
            src_ref=src.at[peer],
            dst_ref=dst.at[me],
            send_sem=send_sem,
            recv_sem=recv_sem,
            device_id=(to_zone, peer),
            device_id_type=MESH,
        )

    def send_all(src, dst, to_zone, first, send_sem, recv_sem):
        def start(i, carry):
            peer = lax.rem(me + i, PEERS)
            copy_to(src, dst, peer, to_zone, send_sem, recv_sem).start()
            return carry

        lax.fori_loop(first, PEERS, start, 0)

    def all_of(src, dst, to_zone, count, send_sem, recv_sem):
        return pltpu.make_async_remote_copy(
            src_ref=src.at[pl.ds(0, count)],
            dst_ref=dst.at[pl.ds(0, count)],
            send_sem=send_sem,
            recv_sem=recv_sem,
            device_id=(to_zone, lax.rem(me + 1, PEERS)),
            device_id_type=MESH,
        )

    counts = send_count[0].astype(F32)
    lane_row = iota((1, LANES), 1)

    def expand(row, mask):
        return to_int(dot_exact(row, mask))

    lane_half = (iota((96, LANES), 1) >> 2) & 1

    def halves(two):
        return jnp.where(lane_half == 0, two[0:96, :], two[96:192, :])

    def widen(one):
        zero = jnp.zeros((96, LANES), F32)
        return jnp.concatenate(
            [jnp.where(lane_half == 0, one, zero), jnp.where(lane_half == 1, one, zero)], axis=0
        )

    def times(values, hot):
        hi, lo = split(values)
        both = dot(jnp.concatenate([hi, lo], axis=0), hot)
        rows = values.shape[0]
        return both[0:rows] + both[rows : 2 * rows]

    def times_t(values, hot):
        hi, lo = split(values)
        both = dot_t(jnp.concatenate([hi, lo], axis=0), hot)
        rows = values.shape[0]
        return both[0:rows] + both[rows : 2 * rows]

    def fluid_ghosts():
        return to_tiles(halves(times(fx[...], f_send[...])))

    def fluid_first():
        for v in range(NV):
            fx[v * COLS : (v + 1) * COLS, :] = adjoint_start[0, :, v * CELLS : (v + 1) * CELLS]
        mask = pick_mask()
        slot = 6 * (lane_row & 3)
        ids = spread_ids(send_rows[0, 0].astype(F32), slot, mask)
        ids = jnp.where(slot < expand(counts, mask), ids, -1)
        f_send[...] = onehot(ids, CELLS)
        ghost_tx[0] = fluid_ghosts()

    def fluid_pair():
        f_cell[...] = onehot(iface_cell[...], CELLS)
        s = iface_slot[...]
        place = ((s >> 3) & 3) * LANES + (s >> 5) * 8 + (s & 7)
        for a in range(4):
            lanes = slice(a * IFACES, (a + 1) * IFACES)
            f_slot[:, lanes] = onehot(place[a : a + 1, :] & (BASE - 1), BASE)
            f_slot_tag[:, lanes] = eight(place[a : a + 1, :] >> 8)
        at = times(fx[...], f_cell[...])
        live = iota((1, IFACES), 1) < iface_count[0]
        heat = flux_out[0:1, :] * at[0:COLS, :]
        for v in range(1, NV):
            heat = heat + flux_out[v : v + 1, :] * at[v * COLS : (v + 1) * COLS, :]
        heat = jnp.where(live, heat, 0.0)
        for a in range(4):
            lanes = slice(a * IFACES, (a + 1) * IFACES)
            hi, lo = split(iface_weight[a : a + 1, :] * heat)
            s_hi[:, lanes] = hi
            s_lo[:, lanes] = lo

        def fetch(off):
            return s_hi[:, pl.ds(off, 1024)], s_lo[:, pl.ds(off, 1024)]

        wide_scatter(fetch, 8, f_slot, f_slot_tag, 1024, 1024, acc)
        rows = [
            jnp.concatenate(
                [acc[2 * q * COLS : (2 * q + 1) * COLS, :], acc[(2 * q + 1) * COLS : (2 * q + 2) * COLS, :]],
                axis=1,
            )
            for q in range(4)
        ]
        pair_tx[...] = to_tiles(jnp.concatenate(rows, axis=0))

    def fluid_prepare():
        left_io = iota((CELLS, 256), 0)
        ghost_io = CELLS + (left_io >> 3) * 4 + (left_io & 3)

        def body(off):
            lanes = pl.ds(off, 256)
            left = jnp.where(left_io == face_left[:, lanes], 1.0, 0.0)
            right = jnp.where(left_io == face_right[:, lanes], 1.0, 0.0)
            ghost = jnp.where(ghost_io == face_right[:, lanes], 1.0, 0.0)
            f_left[:, lanes] = left.astype(BF16)
            f_diff[0:CELLS, lanes] = (left - right).astype(BF16)
            f_diff[CELLS : CELLS + LANES, lanes] = (-ghost).astype(BF16)

        chunked(FACES, 256, body)

    def fluid_faces(off):
        lanes = pl.ds(off, 128)
        left = block_left[:, :, lanes].astype(F32)
        right = block_right[:, :, lanes].astype(F32)
        both = left + right
        jumps = [f_jump[b * COLS : (b + 1) * COLS, lanes] for b in range(NV)]
        for a in range(NV):
            rows = slice(a * COLS, (a + 1) * COLS)
            to_right = right[0, a : a + 1, :] * jumps[0]
            to_both = both[0, a : a + 1, :] * jumps[0]
            for b in range(1, NV):
                to_right = to_right + right[b, a : a + 1, :] * jumps[b]
                to_both = to_both + both[b, a : a + 1, :] * jumps[b]
            f_right[rows, lanes] = to_right
            f_both[rows, lanes] = to_both

    def fluid_out(sweep):
        ghost = widen(from_tiles(ghost_rx[sweep])[0:96, :])
        f_jump[...] = times(fx[...], f_diff[0:CELLS, :]) + times(ghost, f_diff[CELLS:, :])
        chunked(FACES, 128, fluid_faces)
        ghost_image = -times_t(f_right[...], f_diff[CELLS:, :])
        back_tx[sweep] = to_tiles(halves(ghost_image))

    def cell_apply(blocks, values, put):
        for chunk in range(CELLS // 128):
            lanes = slice(chunk * 128, (chunk + 1) * 128)
            taken = blocks[:, :, lanes].astype(F32)
            for a in range(NV):
                total = taken[0, a : a + 1, :] * values[0:COLS, lanes]
                for b in range(1, NV):
                    total = total + taken[b, a : a + 1, :] * values[b * COLS : (b + 1) * COLS, lanes]
                put(slice(a * COLS, (a + 1) * COLS), lanes, total)

    def fluid_own(sweep):
        f_image[...] = times_t(f_both[...], f_left[...]) - times_t(f_right[...], f_diff[0:CELLS, :])

        def put(rows, lanes, total):
            f_image[rows, lanes] += total

        cell_apply(cell_diag, fx, put)

    def fluid_coupling():
        arrived = from_tiles(pair_rx[...])
        blocks = []
        for q in range(4):
            rows = arrived[q * COLS : (q + 1) * COLS, :]
            blocks += [rows[:, 0:BASE], rows[:, BASE:LANES]]
        put_blocks(xh, xl, 0, blocks)

        def put(off, found):
            s_picked[:, pl.ds(off, 1024)] = found

        wide_gather(xh, xl, 8, f_slot, f_slot_tag, 1024, 1024, put)
        live = iota((1, IFACES), 1) < iface_count[0]
        wall = iface_weight[0:1, :] * s_picked[:, 0:IFACES]
        for a in range(1, 4):
            wall = wall + iface_weight[a : a + 1, :] * s_picked[:, a * IFACES : (a + 1) * IFACES]
        wall = jnp.where(live, wall, 0.0)
        added = jnp.concatenate([flux_in[v : v + 1, :] * wall for v in range(NV)], axis=0)
        f_coupling[...] = times_t(added, f_cell[...])

    def fluid_update(sweep):
        returned = widen(from_tiles(back_rx[sweep])[0:96, :])
        f_image[...] += times_t(returned, f_send[...]) + f_coupling[...]
        for v in range(NV):
            rows = slice(v * COLS, (v + 1) * COLS)
            f_image[rows, :] = right_side[0, :, v * CELLS : (v + 1) * CELLS] - f_image[rows, :]

        def put(rows, lanes, total):
            fx[rows, lanes] += total

        cell_apply(cell_prec, f_image, put)

    def fluid_last():
        for v in range(NV):
            rows = slice(v * COLS, (v + 1) * COLS)
            out_x[0, :, v * CELLS : (v + 1) * CELLS] = fx[rows, :]
            out_r[0, :, v * CELLS : (v + 1) * CELLS] = f_image[rows, :]

    def load_own():
        put_blocks(xh, xl, 0, [sx[:, k * BASE : (k + 1) * BASE] for k in range(ROWS // BASE)])

    def list_rows(table, width, counted, hot, tags):
        mask = pick_mask()
        amount = expand(counted, mask)
        values = table.astype(F32)
        for q in range(width // 8):
            slot = q * 8 + (lane_row & 7)
            ids = spread_ids(values, slot, mask)
            lanes = slice(q * LANES, (q + 1) * LANES)
            hot[:, lanes] = onehot(ids & (BASE - 1), BASE)
            tags[:, lanes] = eight(jnp.where(slot < amount, ids >> 8, -1))

    def gather_lists(parts, hot, tags):
        def put(off, found):
            s_wide[:, pl.ds(off, LANES)] = found

        wide_gather(xh, xl, ROWS // BASE, hot, tags, parts * LANES, LANES, put)
        return to_tiles(
            jnp.concatenate([s_wide[:, q * LANES : (q + 1) * LANES] for q in range(parts)], axis=0)
        )

    def scatter_lists(tiles, parts, hot, tags):
        arrived = from_tiles(tiles)
        for q in range(parts):
            lanes = slice(q * LANES, (q + 1) * LANES)
            hi, lo = split(arrived[q * COLS : (q + 1) * COLS, :])
            s_hi[:, lanes] = hi
            s_lo[:, lanes] = lo

        def fetch(off):
            return s_hi[:, pl.ds(off, LANES)], s_lo[:, pl.ds(off, LANES)]

        wide_scatter(fetch, ROWS // BASE, hot, tags, parts * LANES, LANES, acc)

    def solid_first():
        sx[...] = adjoint_start[0]
        load_own()
        list_rows(send_rows[0, 0], GHOST, counts, s_send, s_send_tag)
        ghost_tx[0] = gather_lists(3, s_send, s_send_tag)

    def solid_pair():
        list_rows(iface_nodes[0], SLOTS, iface_pairs[...].astype(F32), s_pair, s_pair_tag)
        pair_tx[...] = gather_lists(4, s_pair, s_pair_tag)

    def solid_prepare():
        live = iota((1, ELEMS), 1) < elem_count[0]

        def one(j, carry):
            ids = s_nodes[j][0:1, :]
            m = ids - ROWS
            p = (m * 2731) >> 16
            g = m - p * GHOST
            ghost = ROWS + (g >> 3) * LANES + p * 8 + (g & 7)
            ids = jnp.where(m >= 0, ghost, ids)
            lanes = pl.ds(pl.multiple_of(j * ELEMS, 128), ELEMS)
            s_elem[:, lanes] = onehot(ids & (BASE - 1), BASE)
            s_elem_tag[:, lanes] = eight(jnp.where(live, ids >> 8, -1))
            mat = elem_mat[j].astype(F32)
            for k in range(NODES // 3):
                s_mat[j, k, 0:3, :] = mat[3 * k : 3 * k + 3, :]
            return carry

        for j in range(NODES):
            s_nodes[j] = eight(elem_nodes[j : j + 1, :])
        lax.fori_loop(0, NODES, one, 0)
        spare = slice(NODES * ELEMS, ELEM_LANES)
        s_elem[:, spare] = jnp.zeros((BASE, ELEMS), BF16)
        s_elem_tag[:, spare] = jnp.full((8, ELEMS), -1, I32)
        s_hi[:, spare] = jnp.zeros((COLS, ELEMS), BF16)
        s_lo[:, spare] = jnp.zeros((COLS, ELEMS), BF16)

    def solid_elements():
        def group(k, carry):
            i0 = k * 3
            for chunk in range(ELEMS // 128):
                lanes = slice(chunk * 128, (chunk + 1) * 128)
                sums = [None, None, None]
                for j in range(NODES):
                    v = s_picked[:, j * ELEMS + chunk * 128 : j * ELEMS + chunk * 128 + 128]
                    for n in range(3):
                        term = s_mat[j, k, n : n + 1, lanes] * v
                        sums[n] = term if j == 0 else sums[n] + term
                for n in range(3):
                    hi, lo = split(sums[n])
                    off = pl.multiple_of((i0 + n) * ELEMS + chunk * 128, 128)
                    s_hi[:, pl.ds(off, 128)] = hi
                    s_lo[:, pl.ds(off, 128)] = lo
            return carry

        lax.fori_loop(0, NODES // 3, group, 0)

    def solid_out(sweep):
        arrived = from_tiles(ghost_rx[sweep])
        blocks = []
        for q in range(3):
            rows = arrived[q * COLS : (q + 1) * COLS, :]
            blocks += [rows[:, 0:BASE], rows[:, BASE:LANES]]
        put_blocks(xh, xl, ROWS // BASE, blocks)

        def put(off, found):
            s_picked[:, pl.ds(off, 768)] = found

        wide_gather(xh, xl, 18, s_elem, s_elem_tag, ELEM_LANES, 768, put)
        solid_elements()

        def fetch(off):
            return s_hi[:, pl.ds(off, 768)], s_lo[:, pl.ds(off, 768)]

        wide_scatter(fetch, 18, s_elem, s_elem_tag, ELEM_LANES, 768, acc)
        rows = [
            jnp.concatenate(
                [
                    acc[(12 + 2 * q) * COLS : (13 + 2 * q) * COLS, :],
                    acc[(13 + 2 * q) * COLS : (14 + 2 * q) * COLS, :],
                ],
                axis=1,
            )
            for q in range(3)
        ]
        back_tx[sweep] = to_tiles(jnp.concatenate(rows, axis=0))

    def solid_own():
        for k in range(ROWS // BASE):
            out_r[0, :, k * BASE : (k + 1) * BASE] = acc[k * COLS : (k + 1) * COLS, :]

    def solid_coupling():
        scatter_lists(pair_rx[...], 4, s_pair, s_pair_tag)
        for k in range(ROWS // BASE):
            s_coupling[:, k * BASE : (k + 1) * BASE] = acc[k * COLS : (k + 1) * COLS, :]

    def solid_update(sweep):
        scatter_lists(back_rx[sweep], 3, s_send, s_send_tag)
        for k in range(ROWS // BASE):
            lanes = slice(k * BASE, (k + 1) * BASE)
            image = out_r[0, :, lanes] + acc[k * COLS : (k + 1) * COLS, :]
            residual = right_side[0, :, lanes] - s_coupling[:, lanes] - image
            out_r[0, :, lanes] = residual
            sx[:, lanes] += node_scale[:, lanes] * residual

    for s in range(SWEEPS):
        ghost_rx[s, me] = jnp.zeros((8, 128), F32)
        back_rx[s, me] = jnp.zeros((8, 128), F32)
    pl.when(is_fluid)(fluid_first)
    pl.when(is_solid)(solid_first)
    pl.semaphore_wait(barrier, 2 * PEERS - 1)
    send_all(ghost_tx.at[0], ghost_rx.at[0], zone, 1, ghost_send_sem.at[0], ghost_recv_sem.at[0])
    pl.when(is_fluid)(fluid_pair)
    pl.when(is_solid)(solid_pair)
    send_all(pair_tx, pair_rx, other, 0, pair_send_sem, pair_recv_sem)
    pl.when(is_fluid)(fluid_prepare)
    pl.when(is_solid)(solid_prepare)

    def sweep_step(s, carry):
        def rest(src, dst, send_sem, recv_sem):
            return all_of(src.at[s], dst.at[s], zone, PEERS - 1, send_sem.at[s], recv_sem.at[s])

        @pl.when(s > 0)
        def _():
            @pl.when(is_fluid)
            def _():
                ghost_tx[s] = fluid_ghosts()

            @pl.when(is_solid)
            def _():
                load_own()
                ghost_tx[s] = gather_lists(3, s_send, s_send_tag)

            send_all(
                ghost_tx.at[s], ghost_rx.at[s], zone, 1, ghost_send_sem.at[s], ghost_recv_sem.at[s]
            )

        rest(ghost_tx, ghost_rx, ghost_send_sem, ghost_recv_sem).wait_recv()
        pl.when(is_fluid)(lambda: fluid_out(s))
        pl.when(is_solid)(lambda: solid_out(s))
        send_all(back_tx.at[s], back_rx.at[s], zone, 1, back_send_sem.at[s], back_recv_sem.at[s])
        pl.when(is_fluid)(lambda: fluid_own(s))
        pl.when(is_solid)(solid_own)

        @pl.when(s == 0)
        def _():
            both = all_of(pair_tx, pair_rx, other, PEERS, pair_send_sem, pair_recv_sem)
            both.wait_recv()
            pl.when(is_fluid)(fluid_coupling)
            pl.when(is_solid)(solid_coupling)
            both.wait_send()

        rest(back_tx, back_rx, back_send_sem, back_recv_sem).wait_recv()
        pl.when(is_fluid)(lambda: fluid_update(s))
        pl.when(is_solid)(lambda: solid_update(s))
        rest(ghost_tx, ghost_rx, ghost_send_sem, ghost_recv_sem).wait_send()
        rest(back_tx, back_rx, back_send_sem, back_recv_sem).wait_send()
        return carry

    lax.fori_loop(0, SWEEPS, sweep_step, 0)

    pl.when(is_fluid)(fluid_last)

    @pl.when(is_solid)
    def _():
        out_x[0] = sx[...]


def on_device(*args):
    flat = (4, 5, 13, 14)
    args = [a.reshape(1, -1) if i in flat else a for i, a in enumerate(args)]
    vmem = pl.BlockSpec(memory_space=pltpu.VMEM)
    smem = pl.BlockSpec(memory_space=pltpu.SMEM)
    specs = [smem if i in (12, 19) else vmem for i in range(len(args))]
    out = jax.ShapeDtypeStruct((1, COLS, ROWS), F32)
    tiles = pltpu.VMEM((SWEEPS, PEERS, 8, 128), F32)
    scratch = [
        tiles,
        tiles,
        tiles,
        tiles,
        pltpu.VMEM((PEERS, 8, 128), F32),
        pltpu.VMEM((PEERS, 8, 128), F32),
        pltpu.VMEM((NV * COLS, CELLS), F32),
        pltpu.VMEM((NV * COLS, CELLS), F32),
        pltpu.VMEM((NV * COLS, CELLS), F32),
        pltpu.VMEM((NV * COLS, FACES), F32),
        pltpu.VMEM((NV * COLS, FACES), F32),
        pltpu.VMEM((NV * COLS, FACES), F32),
        pltpu.VMEM((CELLS + LANES, FACES), BF16),
        pltpu.VMEM((CELLS, FACES), BF16),
        pltpu.VMEM((CELLS, LANES), BF16),
        pltpu.VMEM((CELLS, IFACES), BF16),
        pltpu.VMEM((BASE, 4 * IFACES), BF16),
        pltpu.VMEM((8, 4 * IFACES), I32),
        pltpu.VMEM((COLS, ROWS), F32),
        pltpu.VMEM((COLS, ROWS), F32),
        pltpu.VMEM((NODES, NODES // 3, 8, ELEMS), F32),
        pltpu.VMEM((NODES, 8, ELEMS), I32),
        pltpu.VMEM((BASE, EXTRA), BF16),
        pltpu.VMEM((8, EXTRA), I32),
        pltpu.VMEM((BASE, 4 * LANES), BF16),
        pltpu.VMEM((8, 4 * LANES), I32),
        pltpu.VMEM((BASE, ELEM_LANES), BF16),
        pltpu.VMEM((8, ELEM_LANES), I32),
        pltpu.VMEM((COLS, ELEM_LANES), F32),
        pltpu.VMEM((COLS, ELEM_LANES), BF16),
        pltpu.VMEM((COLS, ELEM_LANES), BF16),
        pltpu.VMEM((COLS, 4 * LANES), F32),
        pltpu.VMEM((18 * COLS, BASE), BF16),
        pltpu.VMEM((18 * COLS, BASE), BF16),
        pltpu.VMEM((18 * COLS, BASE), F32),
        pltpu.SemaphoreType.DMA((SWEEPS,)),
        pltpu.SemaphoreType.DMA((SWEEPS,)),
        pltpu.SemaphoreType.DMA((SWEEPS,)),
        pltpu.SemaphoreType.DMA((SWEEPS,)),
        pltpu.SemaphoreType.DMA,
        pltpu.SemaphoreType.DMA,
    ]
    return pl.pallas_call(
        kernel,
        out_shape=(out, out),
        in_specs=specs,
        out_specs=(vmem, vmem),
        scratch_shapes=scratch,
        compiler_params=pltpu.CompilerParams(
            collective_id=0, has_side_effects=True, vmem_limit_bytes=56 * 1024 * 1024
        ),
    )(*args)


def solution(mesh):
    placed = (
        P("zone", None, "dom"),
        P("zone", None, "dom"),
        P("zone", "dom", None, None),
        P("zone", "dom", None),
        P("dom"),
        P("dom"),
        P(None, None, "dom"),
        P(None, None, "dom"),
        P(None, None, "dom"),
        P(None, None, "dom"),
        P(None, "dom"),
        P(None, None, "dom"),
        P("dom"),
        P("dom"),
        P("dom"),
        P(None, "dom"),
        P(None, "dom"),
        P(None, "dom"),
        P(None, "dom"),
        P("dom"),
        P("dom", None, None),
        P("dom", None),
    )
    return jax.shard_map(
        on_device,
        mesh=mesh,
        in_specs=placed,
        out_specs=(P("zone", None, "dom"), P("zone", None, "dom")),
        check_vma=False,
    )
```

```python
import jax
import jax.numpy as jnp
from jax import lax
from jax.experimental import pallas as pl
from jax.experimental.pallas import tpu as pltpu
from jax.sharding import PartitionSpec as P

MESH = pl.DeviceIdType.MESH
F32 = jnp.float32
BF16 = jnp.bfloat16
I32 = jnp.int32
EXACT = lax.Precision.HIGHEST

SWEEPS = 2
COLS = 32
NV = 6
CELLS = 512
ROWS = 3072
FACES = 1536
ELEMS = 384
NODES = 27
GHOST = 24
SLOTS = 32
IFACES = 256
PEERS = 64
LANES = PEERS * 8
EXTRA = 3 * LANES
ELEM_LANES = 28 * ELEMS
BASE = 256
OWN = ROWS // BASE
ALL = OWN + EXTRA // BASE
STEP = 3584


def hops(step):
    return sum(min(k, 4 - k) for k in step)


FAR_FIRST = sorted(
    ((y, z, x) for y in range(4) for z in range(4) for x in range(4)), key=lambda step: -hops(step)
)
PEER_STEPS = FAR_FIRST[:-1]


def iota(shape, dim):
    return lax.broadcasted_iota(I32, shape, dim)


def dot(a, b):
    return jnp.dot(a, b, preferred_element_type=F32)


def dot_t(a, b):
    return lax.dot_general(a, b, (((1,), (1,)), ((), ())), preferred_element_type=F32)


def dot_exact(a, b):
    return jnp.dot(a, b, precision=EXACT, preferred_element_type=F32)


def split(x):
    hi = x.astype(BF16)
    lo = (x - hi.astype(F32)).astype(BF16)
    return hi, lo


def onehot(ids, count):
    return jnp.where(iota((count, ids.shape[1]), 0) == ids, 1.0, 0.0).astype(BF16)


def onehot_turned(row, count):
    column = eight(row).astype(F32).T[:, 0:1].astype(I32)
    length = row.shape[1]
    return jnp.where(iota((length, count), 1) == column, 1.0, 0.0).astype(BF16)


def eight(row):
    return jnp.broadcast_to(row, (8, row.shape[1]))


def to_int(x):
    return (x + 0.5).astype(I32)


def pick_mask():
    return jnp.where(iota((PEERS, LANES), 0) == (iota((PEERS, LANES), 1) >> 3), 1.0, 0.0)


def spread_ids(table, lane_slot, mask):
    width = table.shape[0]
    chooser = jnp.where(iota((width, LANES), 0) == lane_slot, 1.0, 0.0)
    spread = lax.dot_general(
        table, chooser, (((0,), (0,)), ((), ())), precision=EXACT, preferred_element_type=F32
    )
    return to_int(jnp.sum(spread * mask, axis=0, keepdims=True))


def chunked(total, step, body):
    def run(k, carry):
        body(pl.multiple_of(k * step, 128))
        return carry

    lax.fori_loop(0, total // step, run, 0)


def wide_gather(xh, xl, first, last, hot, tags, total, step, out, add=False):
    def body(off):
        lanes = pl.ds(off, step)
        onto = hot[:, lanes]
        rows = slice(first * COLS, last * COLS)
        found = dot(xh[rows, :], onto) + dot(xl[rows, :], onto)
        tag = tags[:, lanes]
        for g in range(COLS // 8):
            span = slice(g * 8, (g + 1) * 8)
            part = out[span, lanes] if add else jnp.zeros((8, step), F32)
            for a in range(first, last):
                r = (a - first) * COLS + g * 8
                part = jnp.where(tag == a, found[r : r + 8, :], part)
            out[span, lanes] = part

    chunked(total, step, body)


def wide_scatter(his_ref, los_ref, first, last, turned, tags, total, step, acc):
    rows = slice(first * COLS, last * COLS)
    acc[rows, :] = jnp.zeros(((last - first) * COLS, BASE), F32)

    def body(off):
        lanes = pl.ds(off, step)
        hi, lo = his_ref[:, lanes], los_ref[:, lanes]
        onto = turned[lanes, :]
        tag = tags[:, lanes]
        his, los = [], []
        for a in range(first, last):
            m8 = jnp.where(tag == a, 1.0, 0.0)
            m = jnp.concatenate([m8, m8, m8, m8], axis=0).astype(BF16)
            his.append(hi * m)
            los.append(lo * m)
        sum_hi = dot(jnp.concatenate(his, axis=0), onto)
        sum_lo = dot(jnp.concatenate(los, axis=0), onto)
        acc[rows, :] += sum_hi + sum_lo

    chunked(total, step, body)


def put_blocks(xh, xl, first, blocks):
    for k, block in enumerate(blocks):
        rows = slice((first + k) * COLS, (first + k + 1) * COLS)
        hi, lo = split(block)
        xh[rows, :] = hi
        xl[rows, :] = lo


def to_tiles(stacked):
    height = stacked.shape[0]
    if height < 128:
        stacked = jnp.concatenate([stacked, jnp.zeros((128 - height, LANES), F32)], axis=0)
    return stacked.T.reshape(PEERS, 8, 128)


def from_tiles(tiles):
    return tiles.reshape(LANES, 128).T


def kernel(
    adjoint_start,
    right_side,
    send_rows,
    send_count,
    face_left,
    face_right,
    block_left,
    block_right,
    cell_diag,
    cell_prec,
    elem_nodes,
    elem_mat,
    elem_count,
    node_scale,
    iface_cell,
    iface_slot,
    iface_weight,
    flux_in,
    flux_out,
    iface_count,
    iface_nodes,
    iface_pairs,
    out_x,
    out_r,
    ghost_tx,
    ghost_rx,
    back_tx,
    back_rx,
    pair_tx,
    pair_rx,
    fx,
    f_coupling,
    f_image,
    f_jump,
    f_right,
    f_both,
    f_diff,
    f_left,
    f_send,
    f_cell,
    f_slot,
    f_slot_t,
    f_slot_tag,
    sx,
    s_coupling,
    s_mat,
    s_nodes,
    s_send,
    s_send_t,
    s_send_tag,
    s_pair,
    s_pair_t,
    s_pair_tag,
    s_elem,
    s_elem_t,
    s_elem_tag,
    s_picked,
    s_hi,
    s_lo,
    s_wide,
    xh,
    xl,
    acc,
    ghost_send_sem,
    ghost_recv_sem,
    back_send_sem,
    back_recv_sem,
    pair_send_sem,
    pair_recv_sem,
):
    zone = lax.axis_index("zone")
    me = lax.axis_index("dom")
    other = 1 - zone
    is_fluid = zone == 0
    is_solid = zone == 1

    barrier = pltpu.get_barrier_semaphore()

    side = 4
    my, mz, mx = me // (side * side), (me // side) % side, me % side

    def peer_at(step):
        dy, dz, dx = step
        return ((my + dy) % side) * side * side + ((mz + dz) % side) * side + (mx + dx) % side

    for step in FAR_FIRST:
        peer = peer_at(step)
        if step != (0, 0, 0):
            pl.semaphore_signal(barrier, inc=1, device_id=(zone, peer), device_id_type=MESH)
        pl.semaphore_signal(barrier, inc=1, device_id=(other, peer), device_id_type=MESH)

    def copy_to(src, dst, peer, to_zone, send_sem, recv_sem):
        return pltpu.make_async_remote_copy(
            src_ref=src.at[peer],
            dst_ref=dst.at[me],
            send_sem=send_sem,
            recv_sem=recv_sem,
            device_id=(to_zone, peer),
            device_id_type=MESH,
        )

    def send_all(src, dst, to_zone, steps, send_sem, recv_sem):
        for step in steps:
            copy_to(src, dst, peer_at(step), to_zone, send_sem, recv_sem).start()

    def all_of(src, dst, to_zone, count, send_sem, recv_sem):
        return pltpu.make_async_remote_copy(
            src_ref=src.at[pl.ds(0, count)],
            dst_ref=dst.at[pl.ds(0, count)],
            send_sem=send_sem,
            recv_sem=recv_sem,
            device_id=(to_zone, lax.rem(me + 1, PEERS)),
            device_id_type=MESH,
        )

    counts = send_count[0].astype(F32)
    lane_row = iota((1, LANES), 1)

    def expand(row, mask):
        return to_int(dot_exact(row, mask))

    lane_half = (iota((96, LANES), 1) >> 2) & 1

    def halves(two):
        return jnp.where(lane_half == 0, two[0:96, :], two[96:192, :])

    def widen(one):
        zero = jnp.zeros((96, LANES), F32)
        return jnp.concatenate(
            [jnp.where(lane_half == 0, one, zero), jnp.where(lane_half == 1, one, zero)], axis=0
        )

    def times(values, hot):
        hi, lo = split(values)
        both = dot(jnp.concatenate([hi, lo], axis=0), hot)
        rows = values.shape[0]
        return both[0:rows] + both[rows : 2 * rows]

    def times_t(values, hot):
        hi, lo = split(values)
        both = dot_t(jnp.concatenate([hi, lo], axis=0), hot)
        rows = values.shape[0]
        return both[0:rows] + both[rows : 2 * rows]

    def fluid_ghosts():
        return to_tiles(halves(times(fx[...], f_send[...])))

    def fluid_first():
        for v in range(NV):
            fx[v * COLS : (v + 1) * COLS, :] = adjoint_start[0, :, v * CELLS : (v + 1) * CELLS]
        mask = pick_mask()
        slot = 6 * (lane_row & 3)
        ids = spread_ids(send_rows[0, 0].astype(F32), slot, mask)
        ids = jnp.where(slot < expand(counts, mask), ids, -1)
        f_send[...] = onehot(ids, CELLS)
        ghost_tx[0] = fluid_ghosts()

    def fluid_pair():
        f_cell[...] = onehot(iface_cell[...], CELLS)
        s = iface_slot[...]
        place = ((s >> 3) & 3) * LANES + (s >> 5) * 8 + (s & 7)
        for a in range(4):
            lanes = slice(a * IFACES, (a + 1) * IFACES)
            f_slot[:, lanes] = onehot(place[a : a + 1, :] & (BASE - 1), BASE)
            f_slot_t[lanes, :] = onehot_turned(place[a : a + 1, :] & (BASE - 1), BASE)
            f_slot_tag[:, lanes] = eight(place[a : a + 1, :] >> 8)
        at = times(fx[...], f_cell[...])
        live = iota((1, IFACES), 1) < iface_count[0]
        heat = flux_out[0:1, :] * at[0:COLS, :]
        for v in range(1, NV):
            heat = heat + flux_out[v : v + 1, :] * at[v * COLS : (v + 1) * COLS, :]
        heat = jnp.where(live, heat, 0.0)
        for a in range(4):
            lanes = slice(a * IFACES, (a + 1) * IFACES)
            hi, lo = split(iface_weight[a : a + 1, :] * heat)
            s_hi[:, lanes] = hi
            s_lo[:, lanes] = lo

        wide_scatter(s_hi, s_lo, 0, 8, f_slot_t, f_slot_tag, 1024, 1024, acc)
        rows = [
            jnp.concatenate(
                [acc[2 * q * COLS : (2 * q + 1) * COLS, :], acc[(2 * q + 1) * COLS : (2 * q + 2) * COLS, :]],
                axis=1,
            )
            for q in range(4)
        ]
        pair_tx[...] = to_tiles(jnp.concatenate(rows, axis=0))

    def fluid_prepare():
        left_io = iota((CELLS, 128), 0)
        ghost_io = CELLS + (left_io >> 3) * 4 + (left_io & 3)
        for k in range(FACES // 128):
            lanes = slice(k * 128, (k + 1) * 128)
            left = jnp.where(left_io == face_left[k : k + 1, :], 1.0, 0.0)
            right = jnp.where(left_io == face_right[k : k + 1, :], 1.0, 0.0)
            ghost = jnp.where(ghost_io == face_right[k : k + 1, :], 1.0, 0.0)
            f_left[:, lanes] = left.astype(BF16)
            f_diff[0:CELLS, lanes] = (left - right).astype(BF16)
            f_diff[CELLS : CELLS + LANES, lanes] = (-ghost).astype(BF16)

    def fluid_faces(off):
        lanes = pl.ds(off, 128)
        left = block_left[:, :, lanes].astype(F32)
        right = block_right[:, :, lanes].astype(F32)
        both = left + right
        jumps = [f_jump[b * COLS : (b + 1) * COLS, lanes] for b in range(NV)]
        for a in range(NV):
            rows = slice(a * COLS, (a + 1) * COLS)
            to_right = right[0, a : a + 1, :] * jumps[0]
            to_both = both[0, a : a + 1, :] * jumps[0]
            for b in range(1, NV):
                to_right = to_right + right[b, a : a + 1, :] * jumps[b]
                to_both = to_both + both[b, a : a + 1, :] * jumps[b]
            f_right[rows, lanes] = to_right
            f_both[rows, lanes] = to_both

    def fluid_early():
        f_jump[...] = times(fx[...], f_diff[0:CELLS, :])

    def fluid_out(sweep):
        ghost = widen(from_tiles(ghost_rx[sweep])[0:96, :])
        f_jump[...] += times(ghost, f_diff[CELLS:, :])
        chunked(FACES, 128, fluid_faces)
        ghost_image = -times_t(f_right[...], f_diff[CELLS:, :])
        back_tx[sweep] = to_tiles(halves(ghost_image))

    def cell_apply(blocks, values, put):
        for chunk in range(CELLS // 128):
            lanes = slice(chunk * 128, (chunk + 1) * 128)
            taken = blocks[:, :, lanes].astype(F32)
            for a in range(NV):
                total = taken[0, a : a + 1, :] * values[0:COLS, lanes]
                for b in range(1, NV):
                    total = total + taken[b, a : a + 1, :] * values[b * COLS : (b + 1) * COLS, lanes]
                put(slice(a * COLS, (a + 1) * COLS), lanes, total)

    def fluid_own(sweep):
        f_image[...] = times_t(f_both[...], f_left[...]) - times_t(f_right[...], f_diff[0:CELLS, :])

        def put(rows, lanes, total):
            f_image[rows, lanes] += total

        cell_apply(cell_diag, fx, put)

    def fluid_coupling():
        arrived = from_tiles(pair_rx[...])
        blocks = []
        for q in range(4):
            rows = arrived[q * COLS : (q + 1) * COLS, :]
            blocks += [rows[:, 0:BASE], rows[:, BASE:LANES]]
        put_blocks(xh, xl, 0, blocks)

        wide_gather(xh, xl, 0, 8, f_slot, f_slot_tag, 1024, 1024, s_picked)
        live = iota((1, IFACES), 1) < iface_count[0]
        wall = iface_weight[0:1, :] * s_picked[:, 0:IFACES]
        for a in range(1, 4):
            wall = wall + iface_weight[a : a + 1, :] * s_picked[:, a * IFACES : (a + 1) * IFACES]
        wall = jnp.where(live, wall, 0.0)
        added = jnp.concatenate([flux_in[v : v + 1, :] * wall for v in range(NV)], axis=0)
        f_coupling[...] = times_t(added, f_cell[...])

    def fluid_update(sweep):
        returned = widen(from_tiles(back_rx[sweep])[0:96, :])
        f_image[...] += times_t(returned, f_send[...]) + f_coupling[...]
        for v in range(NV):
            rows = slice(v * COLS, (v + 1) * COLS)
            f_image[rows, :] = right_side[0, :, v * CELLS : (v + 1) * CELLS] - f_image[rows, :]

        def put(rows, lanes, total):
            fx[rows, lanes] += total

        cell_apply(cell_prec, f_image, put)

    def fluid_last():
        for v in range(NV):
            rows = slice(v * COLS, (v + 1) * COLS)
            out_x[0, :, v * CELLS : (v + 1) * CELLS] = fx[rows, :]
            out_r[0, :, v * CELLS : (v + 1) * CELLS] = f_image[rows, :]

    def load_own():
        put_blocks(xh, xl, 0, [sx[:, k * BASE : (k + 1) * BASE] for k in range(ROWS // BASE)])

    def list_rows(table, width, counted, hot, turned, tags):
        mask = pick_mask()
        amount = expand(counted, mask)
        values = table.astype(F32)
        for q in range(width // 8):
            slot = q * 8 + (lane_row & 7)
            ids = spread_ids(values, slot, mask)
            lanes = slice(q * LANES, (q + 1) * LANES)
            hot[:, lanes] = onehot(ids & (BASE - 1), BASE)
            turned[lanes, :] = onehot_turned(ids & (BASE - 1), BASE)
            tags[:, lanes] = eight(jnp.where(slot < amount, ids >> 8, -1))

    def gather_lists(parts, hot, tags):
        wide_gather(xh, xl, 0, OWN, hot, tags, parts * LANES, parts * LANES, s_wide)
        return to_tiles(
            jnp.concatenate([s_wide[:, q * LANES : (q + 1) * LANES] for q in range(parts)], axis=0)
        )

    def scatter_lists(tiles, parts, turned, tags):
        arrived = from_tiles(tiles)
        for q in range(parts):
            lanes = slice(q * LANES, (q + 1) * LANES)
            hi, lo = split(arrived[q * COLS : (q + 1) * COLS, :])
            s_hi[:, lanes] = hi
            s_lo[:, lanes] = lo

        wide_scatter(s_hi, s_lo, 0, OWN, turned, tags, parts * LANES, parts * LANES, acc)

    def solid_first():
        sx[...] = adjoint_start[0]
        load_own()
        list_rows(send_rows[0, 0], GHOST, counts, s_send, s_send_t, s_send_tag)
        ghost_tx[0] = gather_lists(3, s_send, s_send_tag)

    def solid_pair():
        list_rows(iface_nodes[0], SLOTS, iface_pairs[...].astype(F32), s_pair, s_pair_t, s_pair_tag)
        pair_tx[...] = gather_lists(4, s_pair, s_pair_tag)

    def solid_prepare():
        live = iota((1, ELEMS), 1) < elem_count[0]

        def one(j, carry):
            ids = s_nodes[j][0:1, :]
            m = ids - ROWS
            p = (m * 2731) >> 16
            g = m - p * GHOST
            ghost = ROWS + (g >> 3) * LANES + p * 8 + (g & 7)
            ids = jnp.where(m >= 0, ghost, ids)
            lanes = pl.ds(pl.multiple_of(j * ELEMS, 128), ELEMS)
            s_elem[:, lanes] = onehot(ids & (BASE - 1), BASE)
            s_elem_t[lanes, :] = onehot_turned(ids & (BASE - 1), BASE)
            s_elem_tag[:, lanes] = eight(jnp.where(live, ids >> 8, -1))
            mat = elem_mat[j].astype(F32)
            for k in range(NODES // 3):
                s_mat[j, k, 0:3, :] = mat[3 * k : 3 * k + 3, :]
            return carry

        for j in range(NODES):
            s_nodes[j] = eight(elem_nodes[j : j + 1, :])
        lax.fori_loop(0, NODES, one, 0)
        spare = slice(NODES * ELEMS, ELEM_LANES)
        s_elem[:, spare] = jnp.zeros((BASE, ELEMS), BF16)
        s_elem_t[spare, :] = jnp.zeros((ELEMS, BASE), BF16)
        s_elem_tag[:, spare] = jnp.full((8, ELEMS), -1, I32)
        s_hi[:, spare] = jnp.zeros((COLS, ELEMS), BF16)
        s_lo[:, spare] = jnp.zeros((COLS, ELEMS), BF16)

    def solid_elements():
        def group(k, carry):
            i0 = k * 3
            for chunk in range(ELEMS // 128):
                lanes = slice(chunk * 128, (chunk + 1) * 128)
                sums = [None, None, None]
                for j in range(NODES):
                    v = s_picked[:, j * ELEMS + chunk * 128 : j * ELEMS + chunk * 128 + 128]
                    for n in range(3):
                        term = s_mat[j, k, n : n + 1, lanes] * v
                        sums[n] = term if j == 0 else sums[n] + term
                for n in range(3):
                    hi, lo = split(sums[n])
                    off = pl.multiple_of((i0 + n) * ELEMS + chunk * 128, 128)
                    s_hi[:, pl.ds(off, 128)] = hi
                    s_lo[:, pl.ds(off, 128)] = lo
            return carry

        lax.fori_loop(0, NODES // 3, group, 0)

    def solid_early():
        wide_gather(xh, xl, 0, OWN, s_elem, s_elem_tag, ELEM_LANES, STEP, s_picked)

    def solid_out(sweep):
        arrived = from_tiles(ghost_rx[sweep])
        blocks = []
        for q in range(3):
            rows = arrived[q * COLS : (q + 1) * COLS, :]
            blocks += [rows[:, 0:BASE], rows[:, BASE:LANES]]
        put_blocks(xh, xl, ROWS // BASE, blocks)

        wide_gather(xh, xl, OWN, ALL, s_elem, s_elem_tag, ELEM_LANES, STEP, s_picked, add=True)
        solid_elements()
        wide_scatter(s_hi, s_lo, OWN, ALL, s_elem_t, s_elem_tag, ELEM_LANES, STEP, acc)
        rows = [
            jnp.concatenate(
                [
                    acc[(12 + 2 * q) * COLS : (13 + 2 * q) * COLS, :],
                    acc[(13 + 2 * q) * COLS : (14 + 2 * q) * COLS, :],
                ],
                axis=1,
            )
            for q in range(3)
        ]
        back_tx[sweep] = to_tiles(jnp.concatenate(rows, axis=0))

    def solid_own():
        wide_scatter(s_hi, s_lo, 0, OWN, s_elem_t, s_elem_tag, ELEM_LANES, STEP, acc)
        for k in range(ROWS // BASE):
            out_r[0, :, k * BASE : (k + 1) * BASE] = acc[k * COLS : (k + 1) * COLS, :]

    def solid_coupling():
        scatter_lists(pair_rx[...], 4, s_pair_t, s_pair_tag)
        for k in range(ROWS // BASE):
            s_coupling[:, k * BASE : (k + 1) * BASE] = acc[k * COLS : (k + 1) * COLS, :]

    def solid_update(sweep):
        scatter_lists(back_rx[sweep], 3, s_send_t, s_send_tag)
        for k in range(ROWS // BASE):
            lanes = slice(k * BASE, (k + 1) * BASE)
            image = out_r[0, :, lanes] + acc[k * COLS : (k + 1) * COLS, :]
            residual = right_side[0, :, lanes] - s_coupling[:, lanes] - image
            out_r[0, :, lanes] = residual
            sx[:, lanes] += node_scale[:, lanes] * residual

    for s in range(SWEEPS):
        ghost_rx[s, me] = jnp.zeros((8, 128), F32)
        back_rx[s, me] = jnp.zeros((8, 128), F32)
    pl.when(is_fluid)(fluid_first)
    pl.when(is_solid)(solid_first)
    pl.when(is_fluid)(fluid_pair)
    pl.when(is_solid)(solid_pair)
    pl.when(is_fluid)(fluid_prepare)
    pl.when(is_solid)(solid_prepare)
    pl.semaphore_wait(barrier, 2 * PEERS - 1)
    send_all(ghost_tx.at[0], ghost_rx.at[0], zone, PEER_STEPS, ghost_send_sem.at[0], ghost_recv_sem.at[0])
    send_all(pair_tx, pair_rx, other, FAR_FIRST, pair_send_sem, pair_recv_sem)

    def sweep_step(s, carry):
        def rest(src, dst, send_sem, recv_sem):
            return all_of(src.at[s], dst.at[s], zone, PEERS - 1, send_sem.at[s], recv_sem.at[s])

        @pl.when(s > 0)
        def _():
            @pl.when(is_fluid)
            def _():
                ghost_tx[s] = fluid_ghosts()

            @pl.when(is_solid)
            def _():
                load_own()
                ghost_tx[s] = gather_lists(3, s_send, s_send_tag)

            send_all(
                ghost_tx.at[s], ghost_rx.at[s], zone, PEER_STEPS, ghost_send_sem.at[s], ghost_recv_sem.at[s]
            )

        pl.when(is_fluid)(fluid_early)
        pl.when(is_solid)(solid_early)
        rest(ghost_tx, ghost_rx, ghost_send_sem, ghost_recv_sem).wait_recv()
        pl.when(is_fluid)(lambda: fluid_out(s))
        pl.when(is_solid)(lambda: solid_out(s))
        send_all(back_tx.at[s], back_rx.at[s], zone, PEER_STEPS, back_send_sem.at[s], back_recv_sem.at[s])
        pl.when(is_fluid)(lambda: fluid_own(s))
        pl.when(is_solid)(solid_own)

        @pl.when(s == 0)
        def _():
            both = all_of(pair_tx, pair_rx, other, PEERS, pair_send_sem, pair_recv_sem)
            both.wait_recv()
            pl.when(is_fluid)(fluid_coupling)
            pl.when(is_solid)(solid_coupling)
            both.wait_send()

        rest(back_tx, back_rx, back_send_sem, back_recv_sem).wait_recv()
        pl.when(is_fluid)(lambda: fluid_update(s))
        pl.when(is_solid)(lambda: solid_update(s))
        rest(ghost_tx, ghost_rx, ghost_send_sem, ghost_recv_sem).wait_send()
        rest(back_tx, back_rx, back_send_sem, back_recv_sem).wait_send()
        return carry

    lax.fori_loop(0, SWEEPS, sweep_step, 0)

    pl.when(is_fluid)(fluid_last)

    @pl.when(is_solid)
    def _():
        out_x[0] = sx[...]


def on_device(*args):
    args = list(args)
    args[2] = args[2].transpose(0, 1, 3, 2)
    args[4] = args[4].reshape(-1, 128)
    args[5] = args[5].reshape(-1, 128)
    args[13] = args[13].reshape(1, -1)
    args[14] = args[14].reshape(1, -1)
    args[20] = args[20].transpose(0, 2, 1)
    vmem = pl.BlockSpec(memory_space=pltpu.VMEM)
    smem = pl.BlockSpec(memory_space=pltpu.SMEM)
    specs = [smem if i in (12, 19) else vmem for i in range(len(args))]
    out = jax.ShapeDtypeStruct((1, COLS, ROWS), F32)
    tiles = pltpu.VMEM((SWEEPS, PEERS, 8, 128), F32)
    scratch = [
        tiles,
        tiles,
        tiles,
        tiles,
        pltpu.VMEM((PEERS, 8, 128), F32),
        pltpu.VMEM((PEERS, 8, 128), F32),
        pltpu.VMEM((NV * COLS, CELLS), F32),
        pltpu.VMEM((NV * COLS, CELLS), F32),
        pltpu.VMEM((NV * COLS, CELLS), F32),
        pltpu.VMEM((NV * COLS, FACES), F32),
        pltpu.VMEM((NV * COLS, FACES), F32),
        pltpu.VMEM((NV * COLS, FACES), F32),
        pltpu.VMEM((CELLS + LANES, FACES), BF16),
        pltpu.VMEM((CELLS, FACES), BF16),
        pltpu.VMEM((CELLS, LANES), BF16),
        pltpu.VMEM((CELLS, IFACES), BF16),
        pltpu.VMEM((BASE, 4 * IFACES), BF16),
        pltpu.VMEM((4 * IFACES, BASE), BF16),
        pltpu.VMEM((8, 4 * IFACES), I32),
        pltpu.VMEM((COLS, ROWS), F32),
        pltpu.VMEM((COLS, ROWS), F32),
        pltpu.VMEM((NODES, NODES // 3, 8, ELEMS), F32),
        pltpu.VMEM((NODES, 8, ELEMS), I32),
        pltpu.VMEM((BASE, EXTRA), BF16),
        pltpu.VMEM((EXTRA, BASE), BF16),
        pltpu.VMEM((8, EXTRA), I32),
        pltpu.VMEM((BASE, 4 * LANES), BF16),
        pltpu.VMEM((4 * LANES, BASE), BF16),
        pltpu.VMEM((8, 4 * LANES), I32),
        pltpu.VMEM((BASE, ELEM_LANES), BF16),
        pltpu.VMEM((ELEM_LANES, BASE), BF16),
        pltpu.VMEM((8, ELEM_LANES), I32),
        pltpu.VMEM((COLS, ELEM_LANES), F32),
        pltpu.VMEM((COLS, ELEM_LANES), BF16),
        pltpu.VMEM((COLS, ELEM_LANES), BF16),
        pltpu.VMEM((COLS, 4 * LANES), F32),
        pltpu.VMEM((18 * COLS, BASE), BF16),
        pltpu.VMEM((18 * COLS, BASE), BF16),
        pltpu.VMEM((18 * COLS, BASE), F32),
        pltpu.SemaphoreType.DMA((SWEEPS,)),
        pltpu.SemaphoreType.DMA((SWEEPS,)),
        pltpu.SemaphoreType.DMA((SWEEPS,)),
        pltpu.SemaphoreType.DMA((SWEEPS,)),
        pltpu.SemaphoreType.DMA,
        pltpu.SemaphoreType.DMA,
    ]
    return pl.pallas_call(
        kernel,
        out_shape=(out, out),
        in_specs=specs,
        out_specs=(vmem, vmem),
        scratch_shapes=scratch,
        compiler_params=pltpu.CompilerParams(
            collective_id=0, has_side_effects=True, vmem_limit_bytes=56 * 1024 * 1024
        ),
    )(*args)


def solution(mesh):
    placed = (
        P("zone", None, "dom"),
        P("zone", None, "dom"),
        P("zone", "dom", None, None),
        P("zone", "dom", None),
        P("dom"),
        P("dom"),
        P(None, None, "dom"),
        P(None, None, "dom"),
        P(None, None, "dom"),
        P(None, None, "dom"),
        P(None, "dom"),
        P(None, None, "dom"),
        P("dom"),
        P("dom"),
        P("dom"),
        P(None, "dom"),
        P(None, "dom"),
        P(None, "dom"),
        P(None, "dom"),
        P("dom"),
        P("dom", None, None),
        P("dom", None),
    )
    return jax.shard_map(
        on_device,
        mesh=mesh,
        in_specs=placed,
        out_specs=(P("zone", None, "dom"), P("zone", None, "dom")),
        check_vma=False,
    )
```

```python
import jax
import jax.numpy as jnp
from jax import lax
from jax.experimental import pallas as pl
from jax.experimental.pallas import tpu as pltpu
from jax.sharding import PartitionSpec as P

MESH = pl.DeviceIdType.MESH
F32 = jnp.float32
BF16 = jnp.bfloat16
I32 = jnp.int32
EXACT = lax.Precision.HIGHEST

SWEEPS = 2
COLS = 32
NV = 6
CELLS = 512
ROWS = 3072
FACES = 1536
ELEMS = 384
NODES = 27
GHOST = 24
SLOTS = 32
IFACES = 256
PEERS = 64
LANES = PEERS * 8
EXTRA = 3 * LANES
ELEM_LANES = 28 * ELEMS
BASE = 256
OWN = ROWS // BASE
ALL = OWN + EXTRA // BASE
STEP = 3584
GROUP = 9


def hops(step):
    return sum(min(k, 4 - k) for k in step)


FAR_FIRST = sorted(
    ((y, z, x) for y in range(4) for z in range(4) for x in range(4)), key=lambda step: -hops(step)
)
PEER_STEPS = FAR_FIRST[:-1]


def iota(shape, dim):
    return lax.broadcasted_iota(I32, shape, dim)


def dot(a, b):
    return jnp.dot(a, b, preferred_element_type=F32)


def dot_t(a, b):
    return lax.dot_general(a, b, (((1,), (1,)), ((), ())), preferred_element_type=F32)


def dot_exact(a, b):
    return jnp.dot(a, b, precision=EXACT, preferred_element_type=F32)


def split(x):
    hi = x.astype(BF16)
    lo = (x - hi.astype(F32)).astype(BF16)
    return hi, lo


def onehot(ids, count):
    return jnp.where(iota((count, ids.shape[1]), 0) == ids, 1.0, 0.0).astype(BF16)


def onehot_turned(row, count):
    column = eight(row).astype(F32).T[:, 0:1].astype(I32)
    length = row.shape[1]
    return jnp.where(iota((length, count), 1) == column, 1.0, 0.0).astype(BF16)


def eight(row):
    return jnp.broadcast_to(row, (8, row.shape[1]))


def to_int(x):
    return (x + 0.5).astype(I32)


def pick_mask():
    return jnp.where(iota((PEERS, LANES), 0) == (iota((PEERS, LANES), 1) >> 3), 1.0, 0.0)


def spread_ids(table, lane_slot, mask):
    width = table.shape[0]
    chooser = jnp.where(iota((width, LANES), 0) == lane_slot, 1.0, 0.0)
    spread = lax.dot_general(
        table, chooser, (((0,), (0,)), ((), ())), precision=EXACT, preferred_element_type=F32
    )
    return to_int(jnp.sum(spread * mask, axis=0, keepdims=True))


def chunked(total, step, body):
    def run(k, carry):
        body(pl.multiple_of(k * step, 128))
        return carry

    lax.fori_loop(0, total // step, run, 0)


def wide_gather(xh, xl, first, last, hot, tags, total, step, out, add=False):
    def body(off):
        lanes = pl.ds(off, step)
        onto = hot[:, lanes]
        rows = slice(first * COLS, last * COLS)
        found = dot(xh[rows, :], onto) + dot(xl[rows, :], onto)
        tag = tags[:, lanes]
        for g in range(COLS // 8):
            span = slice(g * 8, (g + 1) * 8)
            part = out[span, lanes] if add else jnp.zeros((8, step), F32)
            for a in range(first, last):
                r = (a - first) * COLS + g * 8
                part = jnp.where(tag == a, found[r : r + 8, :], part)
            out[span, lanes] = part

    chunked(total, step, body)


def wide_scatter(his_ref, los_ref, first, last, turned, tags, total, step, acc):
    rows = slice(first * COLS, last * COLS)
    acc[rows, :] = jnp.zeros(((last - first) * COLS, BASE), F32)

    def body(off):
        lanes = pl.ds(off, step)
        hi, lo = his_ref[:, lanes], los_ref[:, lanes]
        onto = turned[lanes, :]
        tag = tags[:, lanes]
        his, los = [], []
        for a in range(first, last):
            m8 = jnp.where(tag == a, 1.0, 0.0)
            m = jnp.concatenate([m8, m8, m8, m8], axis=0).astype(BF16)
            his.append(hi * m)
            los.append(lo * m)
        sum_hi = dot(jnp.concatenate(his, axis=0), onto)
        sum_lo = dot(jnp.concatenate(los, axis=0), onto)
        acc[rows, :] += sum_hi + sum_lo

    chunked(total, step, body)


def put_blocks(xh, xl, first, blocks):
    for k, block in enumerate(blocks):
        rows = slice((first + k) * COLS, (first + k + 1) * COLS)
        hi, lo = split(block)
        xh[rows, :] = hi
        xl[rows, :] = lo


def to_tiles(stacked):
    height = stacked.shape[0]
    if height < 128:
        stacked = jnp.concatenate([stacked, jnp.zeros((128 - height, LANES), F32)], axis=0)
    return stacked.T.reshape(PEERS, 8, 128)


def from_tiles(tiles):
    return tiles.reshape(LANES, 128).T


def kernel(
    adjoint_start,
    right_side,
    send_rows,
    send_count,
    face_left,
    face_right,
    block_left,
    block_right,
    cell_diag,
    cell_prec,
    elem_nodes,
    elem_mat,
    elem_count,
    node_scale,
    iface_cell,
    iface_slot,
    iface_weight,
    flux_in,
    flux_out,
    iface_count,
    iface_nodes,
    iface_pairs,
    out_x,
    out_r,
    ghost_tx,
    ghost_rx,
    back_tx,
    back_rx,
    pair_tx,
    pair_rx,
    fx,
    f_coupling,
    f_image,
    f_jump,
    f_right,
    f_both,
    f_diff,
    f_left,
    f_send,
    f_cell,
    f_slot,
    f_slot_t,
    f_slot_tag,
    sx,
    s_coupling,
    s_mat,
    s_nodes,
    s_send,
    s_send_t,
    s_send_tag,
    s_pair,
    s_pair_t,
    s_pair_tag,
    s_elem,
    s_elem_t,
    s_elem_tag,
    s_picked,
    s_hi,
    s_lo,
    s_wide,
    xh,
    xl,
    acc,
    ghost_send_sem,
    ghost_recv_sem,
    back_send_sem,
    back_recv_sem,
    pair_send_sem,
    pair_recv_sem,
):
    zone = lax.axis_index("zone")
    me = lax.axis_index("dom")
    other = 1 - zone
    is_fluid = zone == 0
    is_solid = zone == 1

    barrier = pltpu.get_barrier_semaphore()

    side = 4
    my, mz, mx = me // (side * side), (me // side) % side, me % side

    def peer_at(step):
        dy, dz, dx = step
        return ((my + dy) % side) * side * side + ((mz + dz) % side) * side + (mx + dx) % side

    for step in FAR_FIRST:
        peer = peer_at(step)
        if step != (0, 0, 0):
            pl.semaphore_signal(barrier, inc=1, device_id=(zone, peer), device_id_type=MESH)
        pl.semaphore_signal(barrier, inc=1, device_id=(other, peer), device_id_type=MESH)

    def copy_to(src, dst, peer, to_zone, send_sem, recv_sem):
        return pltpu.make_async_remote_copy(
            src_ref=src.at[peer],
            dst_ref=dst.at[me],
            send_sem=send_sem,
            recv_sem=recv_sem,
            device_id=(to_zone, peer),
            device_id_type=MESH,
        )

    def send_all(src, dst, to_zone, steps, send_sem, recv_sem):
        for step in steps:
            copy_to(src, dst, peer_at(step), to_zone, send_sem, recv_sem).start()

    def all_of(src, dst, to_zone, count, send_sem, recv_sem):
        return pltpu.make_async_remote_copy(
            src_ref=src.at[pl.ds(0, count)],
            dst_ref=dst.at[pl.ds(0, count)],
            send_sem=send_sem,
            recv_sem=recv_sem,
            device_id=(to_zone, lax.rem(me + 1, PEERS)),
            device_id_type=MESH,
        )

    counts = send_count[0].astype(F32)
    lane_row = iota((1, LANES), 1)

    def expand(row, mask):
        return to_int(dot_exact(row, mask))

    lane_half = (iota((96, LANES), 1) >> 2) & 1

    def halves(two):
        return jnp.where(lane_half == 0, two[0:96, :], two[96:192, :])

    def widen(one):
        zero = jnp.zeros((96, LANES), F32)
        return jnp.concatenate(
            [jnp.where(lane_half == 0, one, zero), jnp.where(lane_half == 1, one, zero)], axis=0
        )

    def times(values, hot):
        hi, lo = split(values)
        both = dot(jnp.concatenate([hi, lo], axis=0), hot)
        rows = values.shape[0]
        return both[0:rows] + both[rows : 2 * rows]

    def times_t(values, hot):
        hi, lo = split(values)
        both = dot_t(jnp.concatenate([hi, lo], axis=0), hot)
        rows = values.shape[0]
        return both[0:rows] + both[rows : 2 * rows]

    def fluid_ghosts():
        return to_tiles(halves(times(fx[...], f_send[...])))

    def fluid_first():
        for v in range(NV):
            fx[v * COLS : (v + 1) * COLS, :] = adjoint_start[0, :, v * CELLS : (v + 1) * CELLS]
        mask = pick_mask()
        slot = 6 * (lane_row & 3)
        ids = spread_ids(send_rows[0, 0].astype(F32), slot, mask)
        ids = jnp.where(slot < expand(counts, mask), ids, -1)
        f_send[...] = onehot(ids, CELLS)
        ghost_tx[0] = fluid_ghosts()

    def fluid_pair():
        f_cell[...] = onehot(iface_cell[...], CELLS)
        s = iface_slot[...]
        place = ((s >> 3) & 3) * LANES + (s >> 5) * 8 + (s & 7)
        for a in range(4):
            lanes = slice(a * IFACES, (a + 1) * IFACES)
            f_slot[:, lanes] = onehot(place[a : a + 1, :] & (BASE - 1), BASE)
            f_slot_t[lanes, :] = onehot_turned(place[a : a + 1, :] & (BASE - 1), BASE)
            f_slot_tag[:, lanes] = eight(place[a : a + 1, :] >> 8)
        at = times(fx[...], f_cell[...])
        live = iota((1, IFACES), 1) < iface_count[0]
        heat = flux_out[0:1, :] * at[0:COLS, :]
        for v in range(1, NV):
            heat = heat + flux_out[v : v + 1, :] * at[v * COLS : (v + 1) * COLS, :]
        heat = jnp.where(live, heat, 0.0)
        for a in range(4):
            lanes = slice(a * IFACES, (a + 1) * IFACES)
            hi, lo = split(iface_weight[a : a + 1, :] * heat)
            s_hi[:, lanes] = hi
            s_lo[:, lanes] = lo

        wide_scatter(s_hi, s_lo, 0, 8, f_slot_t, f_slot_tag, 1024, 1024, acc)
        rows = [
            jnp.concatenate(
                [acc[2 * q * COLS : (2 * q + 1) * COLS, :], acc[(2 * q + 1) * COLS : (2 * q + 2) * COLS, :]],
                axis=1,
            )
            for q in range(4)
        ]
        pair_tx[...] = to_tiles(jnp.concatenate(rows, axis=0))

    def fluid_prepare():
        left_io = iota((CELLS, 128), 0)
        ghost_io = CELLS + (left_io >> 3) * 4 + (left_io & 3)
        for k in range(FACES // 128):
            lanes = slice(k * 128, (k + 1) * 128)
            left = jnp.where(left_io == face_left[k : k + 1, :], 1.0, 0.0)
            right = jnp.where(left_io == face_right[k : k + 1, :], 1.0, 0.0)
            ghost = jnp.where(ghost_io == face_right[k : k + 1, :], 1.0, 0.0)
            f_left[:, lanes] = left.astype(BF16)
            f_diff[0:CELLS, lanes] = (left - right).astype(BF16)
            f_diff[CELLS : CELLS + LANES, lanes] = (-ghost).astype(BF16)

    def fluid_faces(off):
        lanes = pl.ds(off, 128)
        left = block_left[:, :, lanes].astype(F32)
        right = block_right[:, :, lanes].astype(F32)
        both = left + right
        jumps = [f_jump[b * COLS : (b + 1) * COLS, lanes] for b in range(NV)]
        for a in range(NV):
            rows = slice(a * COLS, (a + 1) * COLS)
            to_right = right[0, a : a + 1, :] * jumps[0]
            to_both = both[0, a : a + 1, :] * jumps[0]
            for b in range(1, NV):
                to_right = to_right + right[b, a : a + 1, :] * jumps[b]
                to_both = to_both + both[b, a : a + 1, :] * jumps[b]
            f_right[rows, lanes] = to_right
            f_both[rows, lanes] = to_both

    def fluid_early():
        f_jump[...] = times(fx[...], f_diff[0:CELLS, :])

    def fluid_out(sweep):
        ghost = widen(from_tiles(ghost_rx[sweep])[0:96, :])
        f_jump[...] += times(ghost, f_diff[CELLS:, :])
        chunked(FACES, 128, fluid_faces)
        ghost_image = -times_t(f_right[...], f_diff[CELLS:, :])
        back_tx[sweep] = to_tiles(halves(ghost_image))

    def cell_apply(blocks, values, put):
        for chunk in range(CELLS // 128):
            lanes = slice(chunk * 128, (chunk + 1) * 128)
            taken = blocks[:, :, lanes].astype(F32)
            for a in range(NV):
                total = taken[0, a : a + 1, :] * values[0:COLS, lanes]
                for b in range(1, NV):
                    total = total + taken[b, a : a + 1, :] * values[b * COLS : (b + 1) * COLS, lanes]
                put(slice(a * COLS, (a + 1) * COLS), lanes, total)

    def fluid_own(sweep):
        f_image[...] = times_t(f_both[...], f_left[...]) - times_t(f_right[...], f_diff[0:CELLS, :])

        def put(rows, lanes, total):
            f_image[rows, lanes] += total

        cell_apply(cell_diag, fx, put)

    def fluid_coupling():
        arrived = from_tiles(pair_rx[...])
        blocks = []
        for q in range(4):
            rows = arrived[q * COLS : (q + 1) * COLS, :]
            blocks += [rows[:, 0:BASE], rows[:, BASE:LANES]]
        put_blocks(xh, xl, 0, blocks)

        wide_gather(xh, xl, 0, 8, f_slot, f_slot_tag, 1024, 1024, s_picked)
        live = iota((1, IFACES), 1) < iface_count[0]
        wall = iface_weight[0:1, :] * s_picked[:, 0:IFACES]
        for a in range(1, 4):
            wall = wall + iface_weight[a : a + 1, :] * s_picked[:, a * IFACES : (a + 1) * IFACES]
        wall = jnp.where(live, wall, 0.0)
        added = jnp.concatenate([flux_in[v : v + 1, :] * wall for v in range(NV)], axis=0)
        f_coupling[...] = times_t(added, f_cell[...])

    def fluid_update(sweep):
        returned = widen(from_tiles(back_rx[sweep])[0:96, :])
        f_image[...] += times_t(returned, f_send[...]) + f_coupling[...]
        for v in range(NV):
            rows = slice(v * COLS, (v + 1) * COLS)
            f_image[rows, :] = right_side[0, :, v * CELLS : (v + 1) * CELLS] - f_image[rows, :]

        def put(rows, lanes, total):
            fx[rows, lanes] += total

        cell_apply(cell_prec, f_image, put)

    def fluid_last():
        for v in range(NV):
            rows = slice(v * COLS, (v + 1) * COLS)
            out_x[0, :, v * CELLS : (v + 1) * CELLS] = fx[rows, :]
            out_r[0, :, v * CELLS : (v + 1) * CELLS] = f_image[rows, :]

    def load_own():
        put_blocks(xh, xl, 0, [sx[:, k * BASE : (k + 1) * BASE] for k in range(ROWS // BASE)])

    def list_rows(table, width, counted, hot, turned, tags):
        mask = pick_mask()
        amount = expand(counted, mask)
        values = table.astype(F32)
        for q in range(width // 8):
            slot = q * 8 + (lane_row & 7)
            ids = spread_ids(values, slot, mask)
            lanes = slice(q * LANES, (q + 1) * LANES)
            hot[:, lanes] = onehot(ids & (BASE - 1), BASE)
            turned[lanes, :] = onehot_turned(ids & (BASE - 1), BASE)
            tags[:, lanes] = eight(jnp.where(slot < amount, ids >> 8, -1))

    def gather_lists(parts, hot, tags):
        wide_gather(xh, xl, 0, OWN, hot, tags, parts * LANES, parts * LANES, s_wide)
        return to_tiles(
            jnp.concatenate([s_wide[:, q * LANES : (q + 1) * LANES] for q in range(parts)], axis=0)
        )

    def scatter_lists(tiles, parts, turned, tags):
        arrived = from_tiles(tiles)
        for q in range(parts):
            lanes = slice(q * LANES, (q + 1) * LANES)
            hi, lo = split(arrived[q * COLS : (q + 1) * COLS, :])
            s_hi[:, lanes] = hi
            s_lo[:, lanes] = lo

        wide_scatter(s_hi, s_lo, 0, OWN, turned, tags, parts * LANES, parts * LANES, acc)

    def solid_first():
        sx[...] = adjoint_start[0]
        load_own()
        list_rows(send_rows[0, 0], GHOST, counts, s_send, s_send_t, s_send_tag)
        ghost_tx[0] = gather_lists(3, s_send, s_send_tag)

    def solid_pair():
        list_rows(iface_nodes[0], SLOTS, iface_pairs[...].astype(F32), s_pair, s_pair_t, s_pair_tag)
        pair_tx[...] = gather_lists(4, s_pair, s_pair_tag)

    def solid_prepare():
        live = iota((1, ELEMS), 1) < elem_count[0]
        ids = elem_nodes[...]
        m = ids - ROWS
        p = (m * 2731) >> 16
        g = m - p * GHOST
        ids = jnp.where(m >= 0, ROWS + (g >> 3) * LANES + p * 8 + (g & 7), ids)
        low = ids & (BASE - 1)
        high = jnp.where(live, ids >> 8, -1)
        for j in range(NODES):
            s_nodes[j] = eight(low[j : j + 1, :])
            s_elem_tag[:, j * ELEMS : (j + 1) * ELEMS] = eight(high[j : j + 1, :])

        def one(j, carry):
            lanes = pl.ds(pl.multiple_of(j * ELEMS, 128), ELEMS)
            s_elem[:, lanes] = onehot(s_nodes[j][0:1, :], BASE)
            mat = elem_mat[j].astype(F32)
            for k in range(NODES // GROUP):
                s_mat[j, k, 0:GROUP, :] = mat[GROUP * k : GROUP * k + GROUP, :]
            return carry

        lax.fori_loop(0, NODES, one, 0, unroll=3)
        padded = jnp.concatenate([low.astype(F32), jnp.zeros((5, ELEMS), F32)], axis=0)
        columns = padded.T.astype(I32)
        for j in range(NODES):
            s_elem_t[j * ELEMS : (j + 1) * ELEMS, :] = jnp.where(
                iota((ELEMS, BASE), 1) == columns[:, j : j + 1], 1.0, 0.0
            ).astype(BF16)
        spare = slice(NODES * ELEMS, ELEM_LANES)
        s_elem[:, spare] = jnp.zeros((BASE, ELEMS), BF16)
        s_elem_t[spare, :] = jnp.zeros((ELEMS, BASE), BF16)
        s_elem_tag[:, spare] = jnp.full((8, ELEMS), -1, I32)
        s_hi[:, spare] = jnp.zeros((COLS, ELEMS), BF16)
        s_lo[:, spare] = jnp.zeros((COLS, ELEMS), BF16)

    def solid_elements():
        def group(k, carry):
            i0 = k * GROUP
            for chunk in range(ELEMS // 128):
                lanes = slice(chunk * 128, (chunk + 1) * 128)
                sums = [None] * GROUP
                for j in range(NODES):
                    v = s_picked[:, j * ELEMS + chunk * 128 : j * ELEMS + chunk * 128 + 128]
                    for n in range(GROUP):
                        term = s_mat[j, k, n : n + 1, lanes] * v
                        sums[n] = term if j == 0 else sums[n] + term
                for n in range(GROUP):
                    hi, lo = split(sums[n])
                    off = pl.multiple_of((i0 + n) * ELEMS + chunk * 128, 128)
                    s_hi[:, pl.ds(off, 128)] = hi
                    s_lo[:, pl.ds(off, 128)] = lo
            return carry

        lax.fori_loop(0, NODES // GROUP, group, 0)

    def solid_early():
        wide_gather(xh, xl, 0, OWN, s_elem, s_elem_tag, ELEM_LANES, STEP, s_picked)

    def solid_out(sweep):
        arrived = from_tiles(ghost_rx[sweep])
        blocks = []
        for q in range(3):
            rows = arrived[q * COLS : (q + 1) * COLS, :]
            blocks += [rows[:, 0:BASE], rows[:, BASE:LANES]]
        put_blocks(xh, xl, ROWS // BASE, blocks)

        wide_gather(xh, xl, OWN, ALL, s_elem, s_elem_tag, ELEM_LANES, STEP, s_picked, add=True)
        solid_elements()
        wide_scatter(s_hi, s_lo, OWN, ALL, s_elem_t, s_elem_tag, ELEM_LANES, STEP, acc)
        rows = [
            jnp.concatenate(
                [
                    acc[(12 + 2 * q) * COLS : (13 + 2 * q) * COLS, :],
                    acc[(13 + 2 * q) * COLS : (14 + 2 * q) * COLS, :],
                ],
                axis=1,
            )
            for q in range(3)
        ]
        back_tx[sweep] = to_tiles(jnp.concatenate(rows, axis=0))

    def solid_own():
        wide_scatter(s_hi, s_lo, 0, OWN, s_elem_t, s_elem_tag, ELEM_LANES, STEP, acc)
        for k in range(ROWS // BASE):
            out_r[0, :, k * BASE : (k + 1) * BASE] = acc[k * COLS : (k + 1) * COLS, :]

    def solid_coupling():
        scatter_lists(pair_rx[...], 4, s_pair_t, s_pair_tag)
        for k in range(ROWS // BASE):
            s_coupling[:, k * BASE : (k + 1) * BASE] = acc[k * COLS : (k + 1) * COLS, :]

    def solid_update(sweep):
        scatter_lists(back_rx[sweep], 3, s_send_t, s_send_tag)
        for k in range(ROWS // BASE):
            lanes = slice(k * BASE, (k + 1) * BASE)
            image = out_r[0, :, lanes] + acc[k * COLS : (k + 1) * COLS, :]
            residual = right_side[0, :, lanes] - s_coupling[:, lanes] - image
            out_r[0, :, lanes] = residual
            sx[:, lanes] += node_scale[:, lanes] * residual

    for s in range(SWEEPS):
        ghost_rx[s, me] = jnp.zeros((8, 128), F32)
        back_rx[s, me] = jnp.zeros((8, 128), F32)
    pl.when(is_fluid)(fluid_first)
    pl.when(is_solid)(solid_first)
    pl.when(is_fluid)(fluid_pair)
    pl.when(is_solid)(solid_pair)
    pl.when(is_fluid)(fluid_prepare)
    pl.when(is_solid)(solid_prepare)
    pl.semaphore_wait(barrier, 2 * PEERS - 1)
    send_all(ghost_tx.at[0], ghost_rx.at[0], zone, PEER_STEPS, ghost_send_sem.at[0], ghost_recv_sem.at[0])
    send_all(pair_tx, pair_rx, other, FAR_FIRST, pair_send_sem, pair_recv_sem)

    def sweep_step(s, carry):
        def rest(src, dst, send_sem, recv_sem):
            return all_of(src.at[s], dst.at[s], zone, PEERS - 1, send_sem.at[s], recv_sem.at[s])

        @pl.when(s > 0)
        def _():
            @pl.when(is_fluid)
            def _():
                ghost_tx[s] = fluid_ghosts()

            @pl.when(is_solid)
            def _():
                load_own()
                ghost_tx[s] = gather_lists(3, s_send, s_send_tag)

            send_all(
                ghost_tx.at[s], ghost_rx.at[s], zone, PEER_STEPS, ghost_send_sem.at[s], ghost_recv_sem.at[s]
            )

        pl.when(is_fluid)(fluid_early)
        pl.when(is_solid)(solid_early)
        rest(ghost_tx, ghost_rx, ghost_send_sem, ghost_recv_sem).wait_recv()
        pl.when(is_fluid)(lambda: fluid_out(s))
        pl.when(is_solid)(lambda: solid_out(s))
        send_all(back_tx.at[s], back_rx.at[s], zone, PEER_STEPS, back_send_sem.at[s], back_recv_sem.at[s])
        pl.when(is_fluid)(lambda: fluid_own(s))
        pl.when(is_solid)(solid_own)

        @pl.when(s == 0)
        def _():
            both = all_of(pair_tx, pair_rx, other, PEERS, pair_send_sem, pair_recv_sem)
            both.wait_recv()
            pl.when(is_fluid)(fluid_coupling)
            pl.when(is_solid)(solid_coupling)
            both.wait_send()

        rest(back_tx, back_rx, back_send_sem, back_recv_sem).wait_recv()
        pl.when(is_fluid)(lambda: fluid_update(s))
        pl.when(is_solid)(lambda: solid_update(s))
        rest(ghost_tx, ghost_rx, ghost_send_sem, ghost_recv_sem).wait_send()
        rest(back_tx, back_rx, back_send_sem, back_recv_sem).wait_send()
        return carry

    lax.fori_loop(0, SWEEPS, sweep_step, 0)

    pl.when(is_fluid)(fluid_last)

    @pl.when(is_solid)
    def _():
        out_x[0] = sx[...]


def on_device(*args):
    args = list(args)
    args[2] = args[2].transpose(0, 1, 3, 2)
    args[4] = args[4].reshape(-1, 128)
    args[5] = args[5].reshape(-1, 128)
    args[13] = args[13].reshape(1, -1)
    args[14] = args[14].reshape(1, -1)
    args[20] = args[20].transpose(0, 2, 1)
    vmem = pl.BlockSpec(memory_space=pltpu.VMEM)
    smem = pl.BlockSpec(memory_space=pltpu.SMEM)
    specs = [smem if i in (12, 19) else vmem for i in range(len(args))]
    out = jax.ShapeDtypeStruct((1, COLS, ROWS), F32)
    tiles = pltpu.VMEM((SWEEPS, PEERS, 8, 128), F32)
    scratch = [
        tiles,
        tiles,
        tiles,
        tiles,
        pltpu.VMEM((PEERS, 8, 128), F32),
        pltpu.VMEM((PEERS, 8, 128), F32),
        pltpu.VMEM((NV * COLS, CELLS), F32),
        pltpu.VMEM((NV * COLS, CELLS), F32),
        pltpu.VMEM((NV * COLS, CELLS), F32),
        pltpu.VMEM((NV * COLS, FACES), F32),
        pltpu.VMEM((NV * COLS, FACES), F32),
        pltpu.VMEM((NV * COLS, FACES), F32),
        pltpu.VMEM((CELLS + LANES, FACES), BF16),
        pltpu.VMEM((CELLS, FACES), BF16),
        pltpu.VMEM((CELLS, LANES), BF16),
        pltpu.VMEM((CELLS, IFACES), BF16),
        pltpu.VMEM((BASE, 4 * IFACES), BF16),
        pltpu.VMEM((4 * IFACES, BASE), BF16),
        pltpu.VMEM((8, 4 * IFACES), I32),
        pltpu.VMEM((COLS, ROWS), F32),
        pltpu.VMEM((COLS, ROWS), F32),
        pltpu.VMEM((NODES, NODES // GROUP, 16, ELEMS), F32),
        pltpu.VMEM((NODES, 8, ELEMS), I32),
        pltpu.VMEM((BASE, EXTRA), BF16),
        pltpu.VMEM((EXTRA, BASE), BF16),
        pltpu.VMEM((8, EXTRA), I32),
        pltpu.VMEM((BASE, 4 * LANES), BF16),
        pltpu.VMEM((4 * LANES, BASE), BF16),
        pltpu.VMEM((8, 4 * LANES), I32),
        pltpu.VMEM((BASE, ELEM_LANES), BF16),
        pltpu.VMEM((ELEM_LANES, BASE), BF16),
        pltpu.VMEM((8, ELEM_LANES), I32),
        pltpu.VMEM((COLS, ELEM_LANES), F32),
        pltpu.VMEM((COLS, ELEM_LANES), BF16),
        pltpu.VMEM((COLS, ELEM_LANES), BF16),
        pltpu.VMEM((COLS, 4 * LANES), F32),
        pltpu.VMEM((18 * COLS, BASE), BF16),
        pltpu.VMEM((18 * COLS, BASE), BF16),
        pltpu.VMEM((18 * COLS, BASE), F32),
        pltpu.SemaphoreType.DMA((SWEEPS,)),
        pltpu.SemaphoreType.DMA((SWEEPS,)),
        pltpu.SemaphoreType.DMA((SWEEPS,)),
        pltpu.SemaphoreType.DMA((SWEEPS,)),
        pltpu.SemaphoreType.DMA,
        pltpu.SemaphoreType.DMA,
    ]
    return pl.pallas_call(
        kernel,
        out_shape=(pltpu.VMEM((1, COLS, ROWS), F32), pltpu.VMEM((1, COLS, ROWS), F32)),
        in_specs=specs,
        out_specs=(vmem, vmem),
        scratch_shapes=scratch,
        compiler_params=pltpu.CompilerParams(
            collective_id=0, has_side_effects=True, vmem_limit_bytes=56 * 1024 * 1024
        ),
    )(*args)


def solution(mesh):
    placed = (
        P("zone", None, "dom"),
        P("zone", None, "dom"),
        P("zone", "dom", None, None),
        P("zone", "dom", None),
        P("dom"),
        P("dom"),
        P(None, None, "dom"),
        P(None, None, "dom"),
        P(None, None, "dom"),
        P(None, None, "dom"),
        P(None, "dom"),
        P(None, None, "dom"),
        P("dom"),
        P("dom"),
        P("dom"),
        P(None, "dom"),
        P(None, "dom"),
        P(None, "dom"),
        P(None, "dom"),
        P("dom"),
        P("dom", None, None),
        P("dom", None),
    )
    return jax.shard_map(
        on_device,
        mesh=mesh,
        in_specs=placed,
        out_specs=(P("zone", None, "dom"), P("zone", None, "dom")),
        check_vma=False,
    )
```

```python
import jax
import jax.numpy as jnp
from jax import lax
from jax.experimental import pallas as pl
from jax.experimental.pallas import tpu as pltpu
from jax.sharding import PartitionSpec as P

MESH = pl.DeviceIdType.MESH
F32 = jnp.float32
BF16 = jnp.bfloat16
I32 = jnp.int32
EXACT = lax.Precision.HIGHEST

SWEEPS = 2
COLS = 32
NV = 6
CELLS = 512
ROWS = 3072
FACES = 1536
ELEMS = 384
NODES = 27
GHOST = 24
SLOTS = 32
IFACES = 256
PEERS = 64
LANES = PEERS * 8
EXTRA = 3 * LANES
ELEM_LANES = 28 * ELEMS
BASE = 256
OWN = ROWS // BASE
ALL = OWN + EXTRA // BASE
STEP = 3584
GROUP = 9


def hops(step):
    return sum(min(k, 4 - k) for k in step)


FAR_FIRST = sorted(
    ((y, z, x) for y in range(4) for z in range(4) for x in range(4)), key=lambda step: -hops(step)
)
PEER_STEPS = FAR_FIRST[:-1]


def iota(shape, dim):
    return lax.broadcasted_iota(I32, shape, dim)


def dot(a, b):
    return jnp.dot(a, b, preferred_element_type=F32)


def dot_t(a, b):
    return lax.dot_general(a, b, (((1,), (1,)), ((), ())), preferred_element_type=F32)


def dot_exact(a, b):
    return jnp.dot(a, b, precision=EXACT, preferred_element_type=F32)


def split(x):
    hi = x.astype(BF16)
    lo = (x - hi.astype(F32)).astype(BF16)
    return hi, lo


def onehot(ids, count):
    return jnp.where(iota((count, ids.shape[1]), 0) == ids, 1.0, 0.0).astype(BF16)


def onehot_turned(row, count):
    column = eight(row).astype(F32).T[:, 0:1].astype(I32)
    length = row.shape[1]
    return jnp.where(iota((length, count), 1) == column, 1.0, 0.0).astype(BF16)


def eight(row):
    return jnp.broadcast_to(row, (8, row.shape[1]))


def to_int(x):
    return (x + 0.5).astype(I32)


def pick_mask():
    return jnp.where(iota((PEERS, LANES), 0) == (iota((PEERS, LANES), 1) >> 3), 1.0, 0.0)


def spread_ids(table, lane_slot, mask):
    width = table.shape[0]
    chooser = jnp.where(iota((width, LANES), 0) == lane_slot, 1.0, 0.0)
    spread = lax.dot_general(
        table, chooser, (((0,), (0,)), ((), ())), precision=EXACT, preferred_element_type=F32
    )
    return to_int(jnp.sum(spread * mask, axis=0, keepdims=True))


def chunked(total, step, body):
    def run(k, carry):
        body(pl.multiple_of(k * step, 128))
        return carry

    lax.fori_loop(0, total // step, run, 0)


def wide_gather(xh, xl, first, last, hot, tags, total, step, out, add=False):
    def body(off):
        lanes = pl.ds(off, step)
        onto = hot[:, lanes]
        rows = slice(first * COLS, last * COLS)
        found = dot(xh[rows, :], onto) + dot(xl[rows, :], onto)
        tag = tags[:, lanes]
        for g in range(COLS // 8):
            span = slice(g * 8, (g + 1) * 8)
            part = out[span, lanes] if add else jnp.zeros((8, step), F32)
            for a in range(first, last):
                r = (a - first) * COLS + g * 8
                part = jnp.where(tag == a, found[r : r + 8, :], part)
            out[span, lanes] = part

    chunked(total, step, body)


def wide_scatter(his_ref, los_ref, first, last, turned, tags, total, step, acc):
    rows = slice(first * COLS, last * COLS)
    acc[rows, :] = jnp.zeros(((last - first) * COLS, BASE), F32)

    def body(off):
        lanes = pl.ds(off, step)
        hi, lo = his_ref[:, lanes], los_ref[:, lanes]
        onto = turned[lanes, :]
        tag = tags[:, lanes]
        his, los = [], []
        for a in range(first, last):
            m8 = jnp.where(tag == a, 1.0, 0.0)
            m = jnp.concatenate([m8, m8, m8, m8], axis=0).astype(BF16)
            his.append(hi * m)
            los.append(lo * m)
        sum_hi = dot(jnp.concatenate(his, axis=0), onto)
        sum_lo = dot(jnp.concatenate(los, axis=0), onto)
        acc[rows, :] += sum_hi + sum_lo

    chunked(total, step, body)


def put_blocks(xh, xl, first, blocks):
    for k, block in enumerate(blocks):
        rows = slice((first + k) * COLS, (first + k + 1) * COLS)
        hi, lo = split(block)
        xh[rows, :] = hi
        xl[rows, :] = lo


def to_tiles(stacked):
    height = stacked.shape[0]
    if height < 128:
        stacked = jnp.concatenate([stacked, jnp.zeros((128 - height, LANES), F32)], axis=0)
    return stacked.T.reshape(PEERS, 8, 128)


def from_tiles(tiles):
    return tiles.reshape(LANES, 128).T


def kernel(
    adjoint_start,
    right_side,
    send_rows,
    send_count,
    face_left,
    face_right,
    block_left,
    block_right,
    cell_diag,
    cell_prec,
    elem_nodes,
    elem_mat,
    elem_count,
    node_scale,
    iface_cell,
    iface_slot,
    iface_weight,
    flux_in,
    flux_out,
    iface_count,
    iface_nodes,
    iface_pairs,
    out_x,
    out_r,
    ghost_tx,
    ghost_rx,
    back_tx,
    back_rx,
    pair_tx,
    pair_rx,
    fx,
    f_coupling,
    f_image,
    f_jump,
    f_right,
    f_both,
    f_diff,
    f_left,
    f_send,
    f_cell,
    f_slot,
    f_slot_t,
    f_slot_tag,
    sx,
    s_coupling,
    s_mat,
    s_nodes,
    s_send,
    s_send_t,
    s_send_tag,
    s_pair,
    s_pair_t,
    s_pair_tag,
    s_elem,
    s_elem_t,
    s_elem_tag,
    s_picked,
    s_hi,
    s_lo,
    s_wide,
    xh,
    xl,
    acc,
    ghost_send_sem,
    ghost_recv_sem,
    back_send_sem,
    back_recv_sem,
    pair_send_sem,
    pair_recv_sem,
):
    zone = lax.axis_index("zone")
    me = lax.axis_index("dom")
    other = 1 - zone
    is_fluid = zone == 0
    is_solid = zone == 1

    barrier = pltpu.get_barrier_semaphore()

    side = 4
    my, mz, mx = me // (side * side), (me // side) % side, me % side

    def peer_at(step):
        dy, dz, dx = step
        return ((my + dy) % side) * side * side + ((mz + dz) % side) * side + (mx + dx) % side

    for step in FAR_FIRST:
        peer = peer_at(step)
        if step != (0, 0, 0):
            pl.semaphore_signal(barrier, inc=1, device_id=(zone, peer), device_id_type=MESH)
        pl.semaphore_signal(barrier, inc=1, device_id=(other, peer), device_id_type=MESH)

    def copy_to(src, dst, peer, to_zone, send_sem, recv_sem):
        return pltpu.make_async_remote_copy(
            src_ref=src.at[peer],
            dst_ref=dst.at[me],
            send_sem=send_sem,
            recv_sem=recv_sem,
            device_id=(to_zone, peer),
            device_id_type=MESH,
        )

    def send_all(src, dst, to_zone, steps, send_sem, recv_sem):
        for step in steps:
            copy_to(src, dst, peer_at(step), to_zone, send_sem, recv_sem).start()

    def all_of(src, dst, to_zone, count, send_sem, recv_sem):
        return pltpu.make_async_remote_copy(
            src_ref=src.at[pl.ds(0, count)],
            dst_ref=dst.at[pl.ds(0, count)],
            send_sem=send_sem,
            recv_sem=recv_sem,
            device_id=(to_zone, lax.rem(me + 1, PEERS)),
            device_id_type=MESH,
        )

    counts = send_count[0].astype(F32)
    lane_row = iota((1, LANES), 1)

    def expand(row, mask):
        return to_int(dot_exact(row, mask))

    lane_half = (iota((96, LANES), 1) >> 2) & 1

    def halves(two):
        return jnp.where(lane_half == 0, two[0:96, :], two[96:192, :])

    def widen(one):
        zero = jnp.zeros((96, LANES), F32)
        return jnp.concatenate(
            [jnp.where(lane_half == 0, one, zero), jnp.where(lane_half == 1, one, zero)], axis=0
        )

    def times(values, hot):
        hi, lo = split(values)
        both = dot(jnp.concatenate([hi, lo], axis=0), hot)
        rows = values.shape[0]
        return both[0:rows] + both[rows : 2 * rows]

    def times_t(values, hot):
        hi, lo = split(values)
        both = dot_t(jnp.concatenate([hi, lo], axis=0), hot)
        rows = values.shape[0]
        return both[0:rows] + both[rows : 2 * rows]

    def fluid_ghosts():
        return to_tiles(halves(times(fx[...], f_send[...])))

    def fluid_first():
        for v in range(NV):
            fx[v * COLS : (v + 1) * COLS, :] = adjoint_start[0, :, v * CELLS : (v + 1) * CELLS]
        mask = pick_mask()
        slot = 6 * (lane_row & 3)
        ids = spread_ids(send_rows[0, 0].astype(F32), slot, mask)
        ids = jnp.where(slot < expand(counts, mask), ids, -1)
        f_send[...] = onehot(ids, CELLS)
        ghost_tx[0] = fluid_ghosts()

    def fluid_pair():
        f_cell[...] = onehot(iface_cell[...], CELLS)
        s = iface_slot[...]
        place = ((s >> 3) & 3) * LANES + (s >> 5) * 8 + (s & 7)
        for a in range(4):
            lanes = slice(a * IFACES, (a + 1) * IFACES)
            f_slot[:, lanes] = onehot(place[a : a + 1, :] & (BASE - 1), BASE)
            f_slot_t[lanes, :] = onehot_turned(place[a : a + 1, :] & (BASE - 1), BASE)
            f_slot_tag[:, lanes] = eight(place[a : a + 1, :] >> 8)
        at = times(fx[...], f_cell[...])
        live = iota((1, IFACES), 1) < iface_count[0]
        heat = flux_out[0:1, :] * at[0:COLS, :]
        for v in range(1, NV):
            heat = heat + flux_out[v : v + 1, :] * at[v * COLS : (v + 1) * COLS, :]
        heat = jnp.where(live, heat, 0.0)
        for a in range(4):
            lanes = slice(a * IFACES, (a + 1) * IFACES)
            hi, lo = split(iface_weight[a : a + 1, :] * heat)
            s_hi[:, lanes] = hi
            s_lo[:, lanes] = lo

        wide_scatter(s_hi, s_lo, 0, 8, f_slot_t, f_slot_tag, 1024, 1024, acc)
        rows = [
            jnp.concatenate(
                [acc[2 * q * COLS : (2 * q + 1) * COLS, :], acc[(2 * q + 1) * COLS : (2 * q + 2) * COLS, :]],
                axis=1,
            )
            for q in range(4)
        ]
        pair_tx[...] = to_tiles(jnp.concatenate(rows, axis=0))

    def fluid_prepare():
        left_io = iota((CELLS, 128), 0)
        ghost_io = CELLS + (left_io >> 3) * 4 + (left_io & 3)
        for k in range(FACES // 128):
            lanes = slice(k * 128, (k + 1) * 128)
            left = jnp.where(left_io == face_left[k : k + 1, :], 1.0, 0.0)
            right = jnp.where(left_io == face_right[k : k + 1, :], 1.0, 0.0)
            ghost = jnp.where(ghost_io == face_right[k : k + 1, :], 1.0, 0.0)
            f_left[:, lanes] = left.astype(BF16)
            f_diff[0:CELLS, lanes] = (left - right).astype(BF16)
            f_diff[CELLS : CELLS + LANES, lanes] = (-ghost).astype(BF16)

    def fluid_faces(off):
        lanes = pl.ds(off, 128)
        left = block_left[:, :, lanes].astype(F32)
        right = block_right[:, :, lanes].astype(F32)
        both = left + right
        jumps = [f_jump[b * COLS : (b + 1) * COLS, lanes] for b in range(NV)]
        for a in range(NV):
            rows = slice(a * COLS, (a + 1) * COLS)
            to_right = right[0, a : a + 1, :] * jumps[0]
            to_both = both[0, a : a + 1, :] * jumps[0]
            for b in range(1, NV):
                to_right = to_right + right[b, a : a + 1, :] * jumps[b]
                to_both = to_both + both[b, a : a + 1, :] * jumps[b]
            f_right[rows, lanes] = to_right
            f_both[rows, lanes] = to_both

    def fluid_early():
        f_jump[...] = times(fx[...], f_diff[0:CELLS, :])

    def fluid_out(sweep):
        ghost = widen(from_tiles(ghost_rx[sweep])[0:96, :])
        f_jump[...] += times(ghost, f_diff[CELLS:, :])
        chunked(FACES, 128, fluid_faces)
        ghost_image = -times_t(f_right[...], f_diff[CELLS:, :])
        back_tx[sweep] = to_tiles(halves(ghost_image))

    def cell_apply(blocks, values, put):
        for chunk in range(CELLS // 128):
            lanes = slice(chunk * 128, (chunk + 1) * 128)
            taken = blocks[:, :, lanes].astype(F32)
            for a in range(NV):
                total = taken[0, a : a + 1, :] * values[0:COLS, lanes]
                for b in range(1, NV):
                    total = total + taken[b, a : a + 1, :] * values[b * COLS : (b + 1) * COLS, lanes]
                put(slice(a * COLS, (a + 1) * COLS), lanes, total)

    def fluid_own(sweep):
        f_image[...] = times_t(f_both[...], f_left[...]) - times_t(f_right[...], f_diff[0:CELLS, :])

        def put(rows, lanes, total):
            f_image[rows, lanes] += total

        cell_apply(cell_diag, fx, put)

    def fluid_coupling():
        arrived = from_tiles(pair_rx[...])
        blocks = []
        for q in range(4):
            rows = arrived[q * COLS : (q + 1) * COLS, :]
            blocks += [rows[:, 0:BASE], rows[:, BASE:LANES]]
        put_blocks(xh, xl, 0, blocks)

        wide_gather(xh, xl, 0, 8, f_slot, f_slot_tag, 1024, 1024, s_picked)
        live = iota((1, IFACES), 1) < iface_count[0]
        wall = iface_weight[0:1, :] * s_picked[:, 0:IFACES]
        for a in range(1, 4):
            wall = wall + iface_weight[a : a + 1, :] * s_picked[:, a * IFACES : (a + 1) * IFACES]
        wall = jnp.where(live, wall, 0.0)
        added = jnp.concatenate([flux_in[v : v + 1, :] * wall for v in range(NV)], axis=0)
        f_coupling[...] = times_t(added, f_cell[...])

    def fluid_update(sweep):
        returned = widen(from_tiles(back_rx[sweep])[0:96, :])
        f_image[...] += times_t(returned, f_send[...]) + f_coupling[...]
        for v in range(NV):
            rows = slice(v * COLS, (v + 1) * COLS)
            f_image[rows, :] = right_side[0, :, v * CELLS : (v + 1) * CELLS] - f_image[rows, :]

        def put(rows, lanes, total):
            fx[rows, lanes] += total

        cell_apply(cell_prec, f_image, put)

    def fluid_last():
        for v in range(NV):
            rows = slice(v * COLS, (v + 1) * COLS)
            out_x[0, :, v * CELLS : (v + 1) * CELLS] = fx[rows, :]
            out_r[0, :, v * CELLS : (v + 1) * CELLS] = f_image[rows, :]

    def load_own():
        put_blocks(xh, xl, 0, [sx[:, k * BASE : (k + 1) * BASE] for k in range(ROWS // BASE)])

    def list_rows(table, width, counted, hot, turned, tags):
        mask = pick_mask()
        amount = expand(counted, mask)
        values = table.astype(F32)
        for q in range(width // 8):
            slot = q * 8 + (lane_row & 7)
            ids = spread_ids(values, slot, mask)
            lanes = slice(q * LANES, (q + 1) * LANES)
            hot[:, lanes] = onehot(ids & (BASE - 1), BASE)
            turned[lanes, :] = onehot_turned(ids & (BASE - 1), BASE)
            tags[:, lanes] = eight(jnp.where(slot < amount, ids >> 8, -1))

    def gather_lists(parts, hot, tags):
        wide_gather(xh, xl, 0, OWN, hot, tags, parts * LANES, parts * LANES, s_wide)
        return to_tiles(
            jnp.concatenate([s_wide[:, q * LANES : (q + 1) * LANES] for q in range(parts)], axis=0)
        )

    def scatter_lists(tiles, parts, turned, tags):
        arrived = from_tiles(tiles)
        for q in range(parts):
            lanes = slice(q * LANES, (q + 1) * LANES)
            hi, lo = split(arrived[q * COLS : (q + 1) * COLS, :])
            s_hi[:, lanes] = hi
            s_lo[:, lanes] = lo

        wide_scatter(s_hi, s_lo, 0, OWN, turned, tags, parts * LANES, parts * LANES, acc)

    def solid_first():
        sx[...] = adjoint_start[0]
        load_own()
        list_rows(send_rows[0, 0], GHOST, counts, s_send, s_send_t, s_send_tag)
        ghost_tx[0] = gather_lists(3, s_send, s_send_tag)

    def solid_pair():
        list_rows(iface_nodes[0], SLOTS, iface_pairs[...].astype(F32), s_pair, s_pair_t, s_pair_tag)
        pair_tx[...] = gather_lists(4, s_pair, s_pair_tag)

    def solid_prepare():
        live = iota((1, ELEMS), 1) < elem_count[0]
        ids = elem_nodes[...]
        m = ids - ROWS
        p = (m * 2731) >> 16
        g = m - p * GHOST
        ids = jnp.where(m >= 0, ROWS + (g >> 3) * LANES + p * 8 + (g & 7), ids)
        low = ids & (BASE - 1)
        high = jnp.where(live, ids >> 8, -1)
        for j in range(NODES):
            s_nodes[j] = eight(low[j : j + 1, :])
            s_elem_tag[:, j * ELEMS : (j + 1) * ELEMS] = eight(high[j : j + 1, :])

        def one(j, carry):
            lanes = pl.ds(pl.multiple_of(j * ELEMS, 128), ELEMS)
            s_elem[:, lanes] = onehot(s_nodes[j][0:1, :], BASE)
            mat = elem_mat[j].astype(F32)
            for k in range(NODES // GROUP):
                s_mat[j, k, 0:GROUP, :] = mat[GROUP * k : GROUP * k + GROUP, :]
            return carry

        lax.fori_loop(0, NODES, one, 0, unroll=3)
        padded = jnp.concatenate([low.astype(F32), jnp.zeros((5, ELEMS), F32)], axis=0)
        columns = padded.T.astype(I32)
        for j in range(NODES):
            s_elem_t[j * ELEMS : (j + 1) * ELEMS, :] = jnp.where(
                iota((ELEMS, BASE), 1) == columns[:, j : j + 1], 1.0, 0.0
            ).astype(BF16)
        spare = slice(NODES * ELEMS, ELEM_LANES)
        s_elem[:, spare] = jnp.zeros((BASE, ELEMS), BF16)
        s_elem_t[spare, :] = jnp.zeros((ELEMS, BASE), BF16)
        s_elem_tag[:, spare] = jnp.full((8, ELEMS), -1, I32)
        s_hi[:, spare] = jnp.zeros((COLS, ELEMS), BF16)
        s_lo[:, spare] = jnp.zeros((COLS, ELEMS), BF16)

    def solid_elements():
        def group(k, carry):
            i0 = k * GROUP
            for chunk in range(ELEMS // 128):
                lanes = slice(chunk * 128, (chunk + 1) * 128)
                sums = [None] * GROUP
                for j in range(NODES):
                    v = s_picked[:, j * ELEMS + chunk * 128 : j * ELEMS + chunk * 128 + 128]
                    for n in range(GROUP):
                        term = s_mat[j, k, n : n + 1, lanes] * v
                        sums[n] = term if j == 0 else sums[n] + term
                for n in range(GROUP):
                    hi, lo = split(sums[n])
                    off = pl.multiple_of((i0 + n) * ELEMS + chunk * 128, 128)
                    s_hi[:, pl.ds(off, 128)] = hi
                    s_lo[:, pl.ds(off, 128)] = lo
            return carry

        lax.fori_loop(0, NODES // GROUP, group, 0)

    def solid_early():
        wide_gather(xh, xl, 0, OWN, s_elem, s_elem_tag, ELEM_LANES, STEP, s_picked)

    def solid_out(sweep):
        arrived = from_tiles(ghost_rx[sweep])
        blocks = []
        for q in range(3):
            rows = arrived[q * COLS : (q + 1) * COLS, :]
            blocks += [rows[:, 0:BASE], rows[:, BASE:LANES]]
        put_blocks(xh, xl, ROWS // BASE, blocks)

        wide_gather(xh, xl, OWN, ALL, s_elem, s_elem_tag, ELEM_LANES, ELEM_LANES // 2, s_picked, add=True)
        solid_elements()
        wide_scatter(s_hi, s_lo, OWN, ALL, s_elem_t, s_elem_tag, ELEM_LANES, ELEM_LANES, acc)
        rows = [
            jnp.concatenate(
                [
                    acc[(12 + 2 * q) * COLS : (13 + 2 * q) * COLS, :],
                    acc[(13 + 2 * q) * COLS : (14 + 2 * q) * COLS, :],
                ],
                axis=1,
            )
            for q in range(3)
        ]
        back_tx[sweep] = to_tiles(jnp.concatenate(rows, axis=0))

    def solid_own():
        wide_scatter(s_hi, s_lo, 0, OWN, s_elem_t, s_elem_tag, ELEM_LANES, STEP, acc)
        for k in range(ROWS // BASE):
            out_r[0, :, k * BASE : (k + 1) * BASE] = acc[k * COLS : (k + 1) * COLS, :]

    def solid_coupling():
        scatter_lists(pair_rx[...], 4, s_pair_t, s_pair_tag)
        for k in range(ROWS // BASE):
            s_coupling[:, k * BASE : (k + 1) * BASE] = acc[k * COLS : (k + 1) * COLS, :]

    def solid_update(sweep):
        scatter_lists(back_rx[sweep], 3, s_send_t, s_send_tag)
        for k in range(ROWS // BASE):
            lanes = slice(k * BASE, (k + 1) * BASE)
            image = out_r[0, :, lanes] + acc[k * COLS : (k + 1) * COLS, :]
            residual = right_side[0, :, lanes] - s_coupling[:, lanes] - image
            out_r[0, :, lanes] = residual
            sx[:, lanes] += node_scale[:, lanes] * residual

    for s in range(SWEEPS):
        ghost_rx[s, me] = jnp.zeros((8, 128), F32)
        back_rx[s, me] = jnp.zeros((8, 128), F32)
    pl.when(is_fluid)(fluid_first)
    pl.when(is_solid)(solid_first)
    pl.when(is_fluid)(fluid_pair)
    pl.when(is_solid)(solid_pair)
    pl.when(is_fluid)(fluid_prepare)
    pl.when(is_solid)(solid_prepare)
    pl.semaphore_wait(barrier, 2 * PEERS - 1)
    send_all(ghost_tx.at[0], ghost_rx.at[0], zone, PEER_STEPS, ghost_send_sem.at[0], ghost_recv_sem.at[0])
    send_all(pair_tx, pair_rx, other, FAR_FIRST, pair_send_sem, pair_recv_sem)

    def sweep_step(s, carry):
        def rest(src, dst, send_sem, recv_sem):
            return all_of(src.at[s], dst.at[s], zone, PEERS - 1, send_sem.at[s], recv_sem.at[s])

        @pl.when(s > 0)
        def _():
            @pl.when(is_fluid)
            def _():
                ghost_tx[s] = fluid_ghosts()

            @pl.when(is_solid)
            def _():
                load_own()
                ghost_tx[s] = gather_lists(3, s_send, s_send_tag)

            send_all(
                ghost_tx.at[s], ghost_rx.at[s], zone, PEER_STEPS, ghost_send_sem.at[s], ghost_recv_sem.at[s]
            )

        pl.when(is_fluid)(fluid_early)
        pl.when(is_solid)(solid_early)
        rest(ghost_tx, ghost_rx, ghost_send_sem, ghost_recv_sem).wait_recv()
        pl.when(is_fluid)(lambda: fluid_out(s))
        pl.when(is_solid)(lambda: solid_out(s))
        send_all(back_tx.at[s], back_rx.at[s], zone, PEER_STEPS, back_send_sem.at[s], back_recv_sem.at[s])
        pl.when(is_fluid)(lambda: fluid_own(s))
        pl.when(is_solid)(solid_own)

        @pl.when(s == 0)
        def _():
            both = all_of(pair_tx, pair_rx, other, PEERS, pair_send_sem, pair_recv_sem)
            both.wait_recv()
            pl.when(is_fluid)(fluid_coupling)
            pl.when(is_solid)(solid_coupling)
            both.wait_send()

        rest(back_tx, back_rx, back_send_sem, back_recv_sem).wait_recv()
        pl.when(is_fluid)(lambda: fluid_update(s))
        pl.when(is_solid)(lambda: solid_update(s))
        rest(ghost_tx, ghost_rx, ghost_send_sem, ghost_recv_sem).wait_send()
        rest(back_tx, back_rx, back_send_sem, back_recv_sem).wait_send()
        return carry

    lax.fori_loop(0, SWEEPS, sweep_step, 0)

    pl.when(is_fluid)(fluid_last)

    @pl.when(is_solid)
    def _():
        out_x[0] = sx[...]


def on_device(*args):
    args = list(args)
    args[2] = args[2].transpose(0, 1, 3, 2)
    args[4] = args[4].reshape(-1, 128)
    args[5] = args[5].reshape(-1, 128)
    args[13] = args[13].reshape(1, -1)
    args[14] = args[14].reshape(1, -1)
    args[20] = args[20].transpose(0, 2, 1)
    vmem = pl.BlockSpec(memory_space=pltpu.VMEM)
    smem = pl.BlockSpec(memory_space=pltpu.SMEM)
    specs = [smem if i in (12, 19) else vmem for i in range(len(args))]
    out = jax.ShapeDtypeStruct((1, COLS, ROWS), F32)
    tiles = pltpu.VMEM((SWEEPS, PEERS, 8, 128), F32)
    scratch = [
        tiles,
        tiles,
        tiles,
        tiles,
        pltpu.VMEM((PEERS, 8, 128), F32),
        pltpu.VMEM((PEERS, 8, 128), F32),
        pltpu.VMEM((NV * COLS, CELLS), F32),
        pltpu.VMEM((NV * COLS, CELLS), F32),
        pltpu.VMEM((NV * COLS, CELLS), F32),
        pltpu.VMEM((NV * COLS, FACES), F32),
        pltpu.VMEM((NV * COLS, FACES), F32),
        pltpu.VMEM((NV * COLS, FACES), F32),
        pltpu.VMEM((CELLS + LANES, FACES), BF16),
        pltpu.VMEM((CELLS, FACES), BF16),
        pltpu.VMEM((CELLS, LANES), BF16),
        pltpu.VMEM((CELLS, IFACES), BF16),
        pltpu.VMEM((BASE, 4 * IFACES), BF16),
        pltpu.VMEM((4 * IFACES, BASE), BF16),
        pltpu.VMEM((8, 4 * IFACES), I32),
        pltpu.VMEM((COLS, ROWS), F32),
        pltpu.VMEM((COLS, ROWS), F32),
        pltpu.VMEM((NODES, NODES // GROUP, 16, ELEMS), F32),
        pltpu.VMEM((NODES, 8, ELEMS), I32),
        pltpu.VMEM((BASE, EXTRA), BF16),
        pltpu.VMEM((EXTRA, BASE), BF16),
        pltpu.VMEM((8, EXTRA), I32),
        pltpu.VMEM((BASE, 4 * LANES), BF16),
        pltpu.VMEM((4 * LANES, BASE), BF16),
        pltpu.VMEM((8, 4 * LANES), I32),
        pltpu.VMEM((BASE, ELEM_LANES), BF16),
        pltpu.VMEM((ELEM_LANES, BASE), BF16),
        pltpu.VMEM((8, ELEM_LANES), I32),
        pltpu.VMEM((COLS, ELEM_LANES), F32),
        pltpu.VMEM((COLS, ELEM_LANES), BF16),
        pltpu.VMEM((COLS, ELEM_LANES), BF16),
        pltpu.VMEM((COLS, 4 * LANES), F32),
        pltpu.VMEM((18 * COLS, BASE), BF16),
        pltpu.VMEM((18 * COLS, BASE), BF16),
        pltpu.VMEM((18 * COLS, BASE), F32),
        pltpu.SemaphoreType.DMA((SWEEPS,)),
        pltpu.SemaphoreType.DMA((SWEEPS,)),
        pltpu.SemaphoreType.DMA((SWEEPS,)),
        pltpu.SemaphoreType.DMA((SWEEPS,)),
        pltpu.SemaphoreType.DMA,
        pltpu.SemaphoreType.DMA,
    ]
    return pl.pallas_call(
        kernel,
        out_shape=(pltpu.VMEM((1, COLS, ROWS), F32), pltpu.VMEM((1, COLS, ROWS), F32)),
        in_specs=specs,
        out_specs=(vmem, vmem),
        scratch_shapes=scratch,
        compiler_params=pltpu.CompilerParams(
            collective_id=0, has_side_effects=True, vmem_limit_bytes=56 * 1024 * 1024
        ),
    )(*args)


def solution(mesh):
    placed = (
        P("zone", None, "dom"),
        P("zone", None, "dom"),
        P("zone", "dom", None, None),
        P("zone", "dom", None),
        P("dom"),
        P("dom"),
        P(None, None, "dom"),
        P(None, None, "dom"),
        P(None, None, "dom"),
        P(None, None, "dom"),
        P(None, "dom"),
        P(None, None, "dom"),
        P("dom"),
        P("dom"),
        P("dom"),
        P(None, "dom"),
        P(None, "dom"),
        P(None, "dom"),
        P(None, "dom"),
        P("dom"),
        P("dom", None, None),
        P("dom", None),
    )
    return jax.shard_map(
        on_device,
        mesh=mesh,
        in_specs=placed,
        out_specs=(P("zone", None, "dom"), P("zone", None, "dom")),
        check_vma=False,
    )
```

```python
import jax
import jax.numpy as jnp
from jax import lax
from jax.experimental import pallas as pl
from jax.experimental.pallas import tpu as pltpu
from jax.sharding import PartitionSpec as P

MESH = pl.DeviceIdType.MESH
F32 = jnp.float32
BF16 = jnp.bfloat16
I32 = jnp.int32
EXACT = lax.Precision.HIGHEST

SWEEPS = 2
COLS = 32
NV = 6
CELLS = 512
ROWS = 3072
FACES = 1536
ELEMS = 384
NODES = 27
GHOST = 24
SLOTS = 32
IFACES = 256
PEERS = 64
LANES = PEERS * 8
EXTRA = 3 * LANES
ELEM_LANES = 28 * ELEMS
BASE = 256
OWN = ROWS // BASE
ALL = OWN + EXTRA // BASE
STEP = 3584
GROUP = 9


def hops(step):
    return sum(min(k, 4 - k) for k in step)


FAR_FIRST = sorted(
    ((y, z, x) for y in range(4) for z in range(4) for x in range(4)), key=lambda step: -hops(step)
)
PEER_STEPS = FAR_FIRST[:-1]


def iota(shape, dim):
    return lax.broadcasted_iota(I32, shape, dim)


def dot(a, b):
    return jnp.dot(a, b, preferred_element_type=F32)


def dot_t(a, b):
    return lax.dot_general(a, b, (((1,), (1,)), ((), ())), preferred_element_type=F32)


def dot_exact(a, b):
    return jnp.dot(a, b, precision=EXACT, preferred_element_type=F32)


def split(x):
    hi = x.astype(BF16)
    lo = (x - hi.astype(F32)).astype(BF16)
    return hi, lo


def onehot(ids, count):
    return jnp.where(iota((count, ids.shape[1]), 0) == ids, 1.0, 0.0).astype(BF16)


def onehot_turned(row, count):
    column = eight(row).astype(F32).T[:, 0:1].astype(I32)
    length = row.shape[1]
    return jnp.where(iota((length, count), 1) == column, 1.0, 0.0).astype(BF16)


def eight(row):
    return jnp.broadcast_to(row, (8, row.shape[1]))


def to_int(x):
    return (x + 0.5).astype(I32)


def pick_mask():
    return jnp.where(iota((PEERS, LANES), 0) == (iota((PEERS, LANES), 1) >> 3), 1.0, 0.0)


def spread_ids(table, lane_slot, mask):
    width = table.shape[0]
    chooser = jnp.where(iota((width, LANES), 0) == lane_slot, 1.0, 0.0)
    spread = lax.dot_general(
        table, chooser, (((0,), (0,)), ((), ())), precision=EXACT, preferred_element_type=F32
    )
    return to_int(jnp.sum(spread * mask, axis=0, keepdims=True))


def chunked(total, step, body):
    def run(k, carry):
        body(pl.multiple_of(k * step, 128))
        return carry

    lax.fori_loop(0, total // step, run, 0)


def wide_gather(xh, xl, first, last, hot, tags, total, step, out, add=False):
    def body(off):
        lanes = pl.ds(off, step)
        onto = hot[:, lanes]
        rows = slice(first * COLS, last * COLS)
        found = dot(xh[rows, :], onto) + dot(xl[rows, :], onto)
        tag = tags[:, lanes]
        for g in range(COLS // 8):
            span = slice(g * 8, (g + 1) * 8)
            part = out[span, lanes] if add else jnp.zeros((8, step), F32)
            for a in range(first, last):
                r = (a - first) * COLS + g * 8
                part = jnp.where(tag == a, found[r : r + 8, :], part)
            out[span, lanes] = part

    chunked(total, step, body)


def wide_scatter(his_ref, los_ref, first, last, turned, tags, total, step, acc):
    rows = slice(first * COLS, last * COLS)
    acc[rows, :] = jnp.zeros(((last - first) * COLS, BASE), F32)

    def body(off):
        lanes = pl.ds(off, step)
        hi, lo = his_ref[:, lanes], los_ref[:, lanes]
        onto = turned[lanes, :]
        tag = tags[:, lanes]
        his, los = [], []
        for a in range(first, last):
            m8 = jnp.where(tag == a, 1.0, 0.0)
            m = jnp.concatenate([m8, m8, m8, m8], axis=0).astype(BF16)
            his.append(hi * m)
            los.append(lo * m)
        sum_hi = dot(jnp.concatenate(his, axis=0), onto)
        sum_lo = dot(jnp.concatenate(los, axis=0), onto)
        acc[rows, :] += sum_hi + sum_lo

    chunked(total, step, body)


def put_blocks(xh, xl, first, blocks):
    for k, block in enumerate(blocks):
        rows = slice((first + k) * COLS, (first + k + 1) * COLS)
        hi, lo = split(block)
        xh[rows, :] = hi
        xl[rows, :] = lo


def to_tiles(stacked):
    height = stacked.shape[0]
    if height < 128:
        stacked = jnp.concatenate([stacked, jnp.zeros((128 - height, LANES), F32)], axis=0)
    return stacked.T.reshape(PEERS, 8, 128)


def from_tiles(tiles):
    return tiles.reshape(LANES, 128).T


def kernel(
    adjoint_start,
    right_side,
    send_rows,
    send_count,
    face_left,
    face_right,
    block_left,
    block_right,
    cell_diag,
    cell_prec,
    elem_nodes,
    elem_mat,
    elem_count,
    node_scale,
    iface_cell,
    iface_slot,
    iface_weight,
    flux_in,
    flux_out,
    iface_count,
    iface_nodes,
    iface_pairs,
    out_x,
    out_r,
    ghost_tx,
    ghost_rx,
    back_tx,
    back_rx,
    pair_tx,
    pair_rx,
    fx,
    f_coupling,
    f_image,
    f_jump,
    f_right,
    f_both,
    f_diff,
    f_left,
    f_send,
    f_cell,
    f_slot,
    f_slot_t,
    f_slot_tag,
    sx,
    s_coupling,
    s_mat,
    s_nodes,
    s_send,
    s_send_t,
    s_send_tag,
    s_pair,
    s_pair_t,
    s_pair_tag,
    s_elem,
    s_elem_t,
    s_elem_tag,
    s_picked,
    s_hi,
    s_lo,
    s_wide,
    xh,
    xl,
    acc,
    ghost_send_sem,
    ghost_recv_sem,
    back_send_sem,
    back_recv_sem,
    pair_send_sem,
    pair_recv_sem,
):
    zone = lax.axis_index("zone")
    me = lax.axis_index("dom")
    other = 1 - zone
    is_fluid = zone == 0
    is_solid = zone == 1

    barrier = pltpu.get_barrier_semaphore()

    side = 4
    my, mz, mx = me // (side * side), (me // side) % side, me % side

    def peer_at(step):
        dy, dz, dx = step
        return ((my + dy) % side) * side * side + ((mz + dz) % side) * side + (mx + dx) % side

    for step in FAR_FIRST:
        peer = peer_at(step)
        if step != (0, 0, 0):
            pl.semaphore_signal(barrier, inc=1, device_id=(zone, peer), device_id_type=MESH)
        pl.semaphore_signal(barrier, inc=1, device_id=(other, peer), device_id_type=MESH)

    def copy_to(src, dst, peer, to_zone, send_sem, recv_sem):
        return pltpu.make_async_remote_copy(
            src_ref=src.at[peer],
            dst_ref=dst.at[me],
            send_sem=send_sem,
            recv_sem=recv_sem,
            device_id=(to_zone, peer),
            device_id_type=MESH,
        )

    def send_all(src, dst, to_zone, steps, send_sem, recv_sem):
        for step in steps:
            copy_to(src, dst, peer_at(step), to_zone, send_sem, recv_sem).start()

    def all_of(src, dst, to_zone, count, send_sem, recv_sem):
        return pltpu.make_async_remote_copy(
            src_ref=src.at[pl.ds(0, count)],
            dst_ref=dst.at[pl.ds(0, count)],
            send_sem=send_sem,
            recv_sem=recv_sem,
            device_id=(to_zone, lax.rem(me + 1, PEERS)),
            device_id_type=MESH,
        )

    counts = send_count[0].astype(F32)
    lane_row = iota((1, LANES), 1)

    def expand(row, mask):
        return to_int(dot_exact(row, mask))

    lane_half = (iota((96, LANES), 1) >> 2) & 1

    def halves(two):
        return jnp.where(lane_half == 0, two[0:96, :], two[96:192, :])

    def widen(one):
        zero = jnp.zeros((96, LANES), F32)
        return jnp.concatenate(
            [jnp.where(lane_half == 0, one, zero), jnp.where(lane_half == 1, one, zero)], axis=0
        )

    def times(values, hot):
        hi, lo = split(values)
        both = dot(jnp.concatenate([hi, lo], axis=0), hot)
        rows = values.shape[0]
        return both[0:rows] + both[rows : 2 * rows]

    def times_t(values, hot):
        hi, lo = split(values)
        both = dot_t(jnp.concatenate([hi, lo], axis=0), hot)
        rows = values.shape[0]
        return both[0:rows] + both[rows : 2 * rows]

    def fluid_ghosts():
        return to_tiles(halves(times(fx[...], f_send[...])))

    def fluid_first():
        for v in range(NV):
            fx[v * COLS : (v + 1) * COLS, :] = adjoint_start[0, :, v * CELLS : (v + 1) * CELLS]
        mask = pick_mask()
        slot = 6 * (lane_row & 3)
        ids = spread_ids(send_rows[0, 0].astype(F32), slot, mask)
        ids = jnp.where(slot < expand(counts, mask), ids, -1)
        f_send[...] = onehot(ids, CELLS)
        ghost_tx[0] = fluid_ghosts()

    def fluid_pair():
        f_cell[...] = onehot(iface_cell[...], CELLS)
        s = iface_slot[...]
        place = ((s >> 3) & 3) * LANES + (s >> 5) * 8 + (s & 7)
        for a in range(4):
            lanes = slice(a * IFACES, (a + 1) * IFACES)
            f_slot[:, lanes] = onehot(place[a : a + 1, :] & (BASE - 1), BASE)
            f_slot_t[lanes, :] = onehot_turned(place[a : a + 1, :] & (BASE - 1), BASE)
            f_slot_tag[:, lanes] = eight(place[a : a + 1, :] >> 8)
        at = times(fx[...], f_cell[...])
        live = iota((1, IFACES), 1) < iface_count[0]
        heat = flux_out[0:1, :] * at[0:COLS, :]
        for v in range(1, NV):
            heat = heat + flux_out[v : v + 1, :] * at[v * COLS : (v + 1) * COLS, :]
        heat = jnp.where(live, heat, 0.0)
        for a in range(4):
            lanes = slice(a * IFACES, (a + 1) * IFACES)
            hi, lo = split(iface_weight[a : a + 1, :] * heat)
            s_hi[:, lanes] = hi
            s_lo[:, lanes] = lo

        wide_scatter(s_hi, s_lo, 0, 8, f_slot_t, f_slot_tag, 1024, 1024, acc)
        rows = [
            jnp.concatenate(
                [acc[2 * q * COLS : (2 * q + 1) * COLS, :], acc[(2 * q + 1) * COLS : (2 * q + 2) * COLS, :]],
                axis=1,
            )
            for q in range(4)
        ]
        pair_tx[...] = to_tiles(jnp.concatenate(rows, axis=0))

    def fluid_prepare():
        left_io = iota((CELLS, 128), 0)
        ghost_io = CELLS + (left_io >> 3) * 4 + (left_io & 3)
        for k in range(FACES // 128):
            lanes = slice(k * 128, (k + 1) * 128)
            left = jnp.where(left_io == face_left[k : k + 1, :], 1.0, 0.0)
            right = jnp.where(left_io == face_right[k : k + 1, :], 1.0, 0.0)
            ghost = jnp.where(ghost_io == face_right[k : k + 1, :], 1.0, 0.0)
            f_left[:, lanes] = left.astype(BF16)
            f_diff[0:CELLS, lanes] = (left - right).astype(BF16)
            f_diff[CELLS : CELLS + LANES, lanes] = (-ghost).astype(BF16)

    def fluid_faces(off):
        lanes = pl.ds(off, 128)
        left = block_left[:, :, lanes].astype(F32)
        right = block_right[:, :, lanes].astype(F32)
        both = left + right
        jumps = [f_jump[b * COLS : (b + 1) * COLS, lanes] for b in range(NV)]
        for a in range(NV):
            rows = slice(a * COLS, (a + 1) * COLS)
            to_right = right[0, a : a + 1, :] * jumps[0]
            to_both = both[0, a : a + 1, :] * jumps[0]
            for b in range(1, NV):
                to_right = to_right + right[b, a : a + 1, :] * jumps[b]
                to_both = to_both + both[b, a : a + 1, :] * jumps[b]
            f_right[rows, lanes] = to_right
            f_both[rows, lanes] = to_both

    def fluid_early():
        f_jump[...] = times(fx[...], f_diff[0:CELLS, :])

    def fluid_out(sweep):
        ghost = widen(from_tiles(ghost_rx[sweep])[0:96, :])
        f_jump[...] += times(ghost, f_diff[CELLS:, :])
        chunked(FACES, 128, fluid_faces)
        ghost_image = -times_t(f_right[...], f_diff[CELLS:, :])
        back_tx[sweep] = to_tiles(halves(ghost_image))

    def cell_apply(blocks, values, put):
        for chunk in range(CELLS // 128):
            lanes = slice(chunk * 128, (chunk + 1) * 128)
            taken = blocks[:, :, lanes].astype(F32)
            for a in range(NV):
                total = taken[0, a : a + 1, :] * values[0:COLS, lanes]
                for b in range(1, NV):
                    total = total + taken[b, a : a + 1, :] * values[b * COLS : (b + 1) * COLS, lanes]
                put(slice(a * COLS, (a + 1) * COLS), lanes, total)

    def fluid_own(sweep):
        f_image[...] = times_t(f_both[...], f_left[...]) - times_t(f_right[...], f_diff[0:CELLS, :])

        def put(rows, lanes, total):
            f_image[rows, lanes] += total

        cell_apply(cell_diag, fx, put)

    def fluid_coupling():
        arrived = from_tiles(pair_rx[...])
        blocks = []
        for q in range(4):
            rows = arrived[q * COLS : (q + 1) * COLS, :]
            blocks += [rows[:, 0:BASE], rows[:, BASE:LANES]]
        put_blocks(xh, xl, 0, blocks)

        wide_gather(xh, xl, 0, 8, f_slot, f_slot_tag, 1024, 1024, s_picked)
        live = iota((1, IFACES), 1) < iface_count[0]
        wall = iface_weight[0:1, :] * s_picked[:, 0:IFACES]
        for a in range(1, 4):
            wall = wall + iface_weight[a : a + 1, :] * s_picked[:, a * IFACES : (a + 1) * IFACES]
        wall = jnp.where(live, wall, 0.0)
        added = jnp.concatenate([flux_in[v : v + 1, :] * wall for v in range(NV)], axis=0)
        f_coupling[...] = times_t(added, f_cell[...])

    def fluid_update(sweep):
        returned = widen(from_tiles(back_rx[sweep])[0:96, :])
        f_image[...] += times_t(returned, f_send[...]) + f_coupling[...]
        for v in range(NV):
            rows = slice(v * COLS, (v + 1) * COLS)
            f_image[rows, :] = right_side[0, :, v * CELLS : (v + 1) * CELLS] - f_image[rows, :]

        def put(rows, lanes, total):
            fx[rows, lanes] += total

        cell_apply(cell_prec, f_image, put)

    def fluid_last():
        for v in range(NV):
            rows = slice(v * COLS, (v + 1) * COLS)
            out_x[0, :, v * CELLS : (v + 1) * CELLS] = fx[rows, :]
            out_r[0, :, v * CELLS : (v + 1) * CELLS] = f_image[rows, :]

    def load_own():
        put_blocks(xh, xl, 0, [sx[:, k * BASE : (k + 1) * BASE] for k in range(ROWS // BASE)])

    def list_rows(table, width, counted, hot, turned, tags):
        mask = pick_mask()
        amount = expand(counted, mask)
        values = table.astype(F32)
        for q in range(width // 8):
            slot = q * 8 + (lane_row & 7)
            ids = spread_ids(values, slot, mask)
            lanes = slice(q * LANES, (q + 1) * LANES)
            hot[:, lanes] = onehot(ids & (BASE - 1), BASE)
            turned[lanes, :] = onehot_turned(ids & (BASE - 1), BASE)
            tags[:, lanes] = eight(jnp.where(slot < amount, ids >> 8, -1))

    def gather_lists(parts, hot, tags):
        wide_gather(xh, xl, 0, OWN, hot, tags, parts * LANES, parts * LANES, s_wide)
        return to_tiles(
            jnp.concatenate([s_wide[:, q * LANES : (q + 1) * LANES] for q in range(parts)], axis=0)
        )

    def scatter_lists(tiles, parts, turned, tags):
        arrived = from_tiles(tiles)
        for q in range(parts):
            lanes = slice(q * LANES, (q + 1) * LANES)
            hi, lo = split(arrived[q * COLS : (q + 1) * COLS, :])
            s_hi[:, lanes] = hi
            s_lo[:, lanes] = lo

        wide_scatter(s_hi, s_lo, 0, OWN, turned, tags, parts * LANES, parts * LANES, acc)

    def solid_first():
        sx[...] = adjoint_start[0]
        load_own()
        list_rows(send_rows[0, 0], GHOST, counts, s_send, s_send_t, s_send_tag)
        ghost_tx[0] = gather_lists(3, s_send, s_send_tag)

    def solid_pair():
        list_rows(iface_nodes[0], SLOTS, iface_pairs[...].astype(F32), s_pair, s_pair_t, s_pair_tag)
        pair_tx[...] = gather_lists(4, s_pair, s_pair_tag)

    def solid_prepare():
        live = iota((1, ELEMS), 1) < elem_count[0]
        ids = elem_nodes[...]
        m = ids - ROWS
        p = (m * 2731) >> 16
        g = m - p * GHOST
        ids = jnp.where(m >= 0, ROWS + (g >> 3) * LANES + p * 8 + (g & 7), ids)
        low = ids & (BASE - 1)
        high = jnp.where(live, ids >> 8, -1)
        for j in range(NODES):
            s_nodes[j] = eight(low[j : j + 1, :])
            s_elem_tag[:, j * ELEMS : (j + 1) * ELEMS] = eight(high[j : j + 1, :])

        def one(j, carry):
            lanes = pl.ds(pl.multiple_of(j * ELEMS, 128), ELEMS)
            s_elem[:, lanes] = onehot(s_nodes[j][0:1, :], BASE)
            mat = elem_mat[j].astype(F32)
            for k in range(NODES // GROUP):
                s_mat[j, k, 0:GROUP, :] = mat[GROUP * k : GROUP * k + GROUP, :]
            return carry

        lax.fori_loop(0, NODES, one, 0, unroll=9)
        padded = jnp.concatenate([low.astype(F32), jnp.zeros((5, ELEMS), F32)], axis=0)
        columns = padded.T.astype(I32)
        for j in range(NODES):
            s_elem_t[j * ELEMS : (j + 1) * ELEMS, :] = jnp.where(
                iota((ELEMS, BASE), 1) == columns[:, j : j + 1], 1.0, 0.0
            ).astype(BF16)
        spare = slice(NODES * ELEMS, ELEM_LANES)
        s_elem[:, spare] = jnp.zeros((BASE, ELEMS), BF16)
        s_elem_t[spare, :] = jnp.zeros((ELEMS, BASE), BF16)
        s_elem_tag[:, spare] = jnp.full((8, ELEMS), -1, I32)
        s_hi[:, spare] = jnp.zeros((COLS, ELEMS), BF16)
        s_lo[:, spare] = jnp.zeros((COLS, ELEMS), BF16)

    def solid_elements():
        def group(k, carry):
            i0 = k * GROUP
            for chunk in range(ELEMS // 128):
                lanes = slice(chunk * 128, (chunk + 1) * 128)
                sums = [None] * GROUP
                for j in range(NODES):
                    v = s_picked[:, j * ELEMS + chunk * 128 : j * ELEMS + chunk * 128 + 128]
                    for n in range(GROUP):
                        term = s_mat[j, k, n : n + 1, lanes] * v
                        sums[n] = term if j == 0 else sums[n] + term
                for n in range(GROUP):
                    hi, lo = split(sums[n])
                    off = pl.multiple_of((i0 + n) * ELEMS + chunk * 128, 128)
                    s_hi[:, pl.ds(off, 128)] = hi
                    s_lo[:, pl.ds(off, 128)] = lo
            return carry

        lax.fori_loop(0, NODES // GROUP, group, 0)

    def solid_early():
        wide_gather(xh, xl, 0, OWN, s_elem, s_elem_tag, ELEM_LANES, STEP, s_picked)

    def solid_out(sweep):
        arrived = from_tiles(ghost_rx[sweep])
        blocks = []
        for q in range(3):
            rows = arrived[q * COLS : (q + 1) * COLS, :]
            blocks += [rows[:, 0:BASE], rows[:, BASE:LANES]]
        put_blocks(xh, xl, ROWS // BASE, blocks)

        wide_gather(xh, xl, OWN, ALL, s_elem, s_elem_tag, ELEM_LANES, ELEM_LANES // 2, s_picked, add=True)
        solid_elements()
        wide_scatter(s_hi, s_lo, OWN, ALL, s_elem_t, s_elem_tag, ELEM_LANES, ELEM_LANES, acc)
        rows = [
            jnp.concatenate(
                [
                    acc[(12 + 2 * q) * COLS : (13 + 2 * q) * COLS, :],
                    acc[(13 + 2 * q) * COLS : (14 + 2 * q) * COLS, :],
                ],
                axis=1,
            )
            for q in range(3)
        ]
        back_tx[sweep] = to_tiles(jnp.concatenate(rows, axis=0))

    def solid_own():
        wide_scatter(s_hi, s_lo, 0, OWN, s_elem_t, s_elem_tag, ELEM_LANES, STEP, acc)
        for k in range(ROWS // BASE):
            out_r[0, :, k * BASE : (k + 1) * BASE] = acc[k * COLS : (k + 1) * COLS, :]

    def solid_coupling():
        scatter_lists(pair_rx[...], 4, s_pair_t, s_pair_tag)
        for k in range(ROWS // BASE):
            s_coupling[:, k * BASE : (k + 1) * BASE] = acc[k * COLS : (k + 1) * COLS, :]

    def solid_update(sweep):
        scatter_lists(back_rx[sweep], 3, s_send_t, s_send_tag)
        for k in range(ROWS // BASE):
            lanes = slice(k * BASE, (k + 1) * BASE)
            image = out_r[0, :, lanes] + acc[k * COLS : (k + 1) * COLS, :]
            residual = right_side[0, :, lanes] - s_coupling[:, lanes] - image
            out_r[0, :, lanes] = residual
            sx[:, lanes] += node_scale[:, lanes] * residual

    for s in range(SWEEPS):
        ghost_rx[s, me] = jnp.zeros((8, 128), F32)
        back_rx[s, me] = jnp.zeros((8, 128), F32)
    pl.when(is_fluid)(fluid_first)
    pl.when(is_solid)(solid_first)
    pl.when(is_fluid)(fluid_prepare)
    pl.when(is_solid)(solid_prepare)
    pl.semaphore_wait(barrier, 2 * PEERS - 1)
    send_all(ghost_tx.at[0], ghost_rx.at[0], zone, PEER_STEPS, ghost_send_sem.at[0], ghost_recv_sem.at[0])
    pl.when(is_fluid)(fluid_pair)
    pl.when(is_solid)(solid_pair)
    send_all(pair_tx, pair_rx, other, FAR_FIRST, pair_send_sem, pair_recv_sem)

    def sweep_step(s, carry):
        def rest(src, dst, send_sem, recv_sem):
            return all_of(src.at[s], dst.at[s], zone, PEERS - 1, send_sem.at[s], recv_sem.at[s])

        @pl.when(s > 0)
        def _():
            @pl.when(is_fluid)
            def _():
                ghost_tx[s] = fluid_ghosts()

            @pl.when(is_solid)
            def _():
                load_own()
                ghost_tx[s] = gather_lists(3, s_send, s_send_tag)

            send_all(
                ghost_tx.at[s], ghost_rx.at[s], zone, PEER_STEPS, ghost_send_sem.at[s], ghost_recv_sem.at[s]
            )

        pl.when(is_fluid)(fluid_early)
        pl.when(is_solid)(solid_early)
        rest(ghost_tx, ghost_rx, ghost_send_sem, ghost_recv_sem).wait_recv()
        pl.when(is_fluid)(lambda: fluid_out(s))
        pl.when(is_solid)(lambda: solid_out(s))
        send_all(back_tx.at[s], back_rx.at[s], zone, PEER_STEPS, back_send_sem.at[s], back_recv_sem.at[s])
        pl.when(is_fluid)(lambda: fluid_own(s))
        pl.when(is_solid)(solid_own)

        @pl.when(s == 0)
        def _():
            both = all_of(pair_tx, pair_rx, other, PEERS, pair_send_sem, pair_recv_sem)
            both.wait_recv()
            pl.when(is_fluid)(fluid_coupling)
            pl.when(is_solid)(solid_coupling)
            both.wait_send()

        rest(back_tx, back_rx, back_send_sem, back_recv_sem).wait_recv()
        pl.when(is_fluid)(lambda: fluid_update(s))
        pl.when(is_solid)(lambda: solid_update(s))
        rest(ghost_tx, ghost_rx, ghost_send_sem, ghost_recv_sem).wait_send()
        rest(back_tx, back_rx, back_send_sem, back_recv_sem).wait_send()
        return carry

    lax.fori_loop(0, SWEEPS, sweep_step, 0)

    pl.when(is_fluid)(fluid_last)

    @pl.when(is_solid)
    def _():
        out_x[0] = sx[...]


def on_device(*args):
    args = list(args)
    args[2] = args[2].transpose(0, 1, 3, 2)
    args[4] = args[4].reshape(-1, 128)
    args[5] = args[5].reshape(-1, 128)
    args[13] = args[13].reshape(1, -1)
    args[14] = args[14].reshape(1, -1)
    args[20] = args[20].transpose(0, 2, 1)
    vmem = pl.BlockSpec(memory_space=pltpu.VMEM)
    smem = pl.BlockSpec(memory_space=pltpu.SMEM)
    specs = [smem if i in (12, 19) else vmem for i in range(len(args))]
    out = jax.ShapeDtypeStruct((1, COLS, ROWS), F32)
    tiles = pltpu.VMEM((SWEEPS, PEERS, 8, 128), F32)
    scratch = [
        tiles,
        tiles,
        tiles,
        tiles,
        pltpu.VMEM((PEERS, 8, 128), F32),
        pltpu.VMEM((PEERS, 8, 128), F32),
        pltpu.VMEM((NV * COLS, CELLS), F32),
        pltpu.VMEM((NV * COLS, CELLS), F32),
        pltpu.VMEM((NV * COLS, CELLS), F32),
        pltpu.VMEM((NV * COLS, FACES), F32),
        pltpu.VMEM((NV * COLS, FACES), F32),
        pltpu.VMEM((NV * COLS, FACES), F32),
        pltpu.VMEM((CELLS + LANES, FACES), BF16),
        pltpu.VMEM((CELLS, FACES), BF16),
        pltpu.VMEM((CELLS, LANES), BF16),
        pltpu.VMEM((CELLS, IFACES), BF16),
        pltpu.VMEM((BASE, 4 * IFACES), BF16),
        pltpu.VMEM((4 * IFACES, BASE), BF16),
        pltpu.VMEM((8, 4 * IFACES), I32),
        pltpu.VMEM((COLS, ROWS), F32),
        pltpu.VMEM((COLS, ROWS), F32),
        pltpu.VMEM((NODES, NODES // GROUP, 16, ELEMS), F32),
        pltpu.VMEM((NODES, 8, ELEMS), I32),
        pltpu.VMEM((BASE, EXTRA), BF16),
        pltpu.VMEM((EXTRA, BASE), BF16),
        pltpu.VMEM((8, EXTRA), I32),
        pltpu.VMEM((BASE, 4 * LANES), BF16),
        pltpu.VMEM((4 * LANES, BASE), BF16),
        pltpu.VMEM((8, 4 * LANES), I32),
        pltpu.VMEM((BASE, ELEM_LANES), BF16),
        pltpu.VMEM((ELEM_LANES, BASE), BF16),
        pltpu.VMEM((8, ELEM_LANES), I32),
        pltpu.VMEM((COLS, ELEM_LANES), F32),
        pltpu.VMEM((COLS, ELEM_LANES), BF16),
        pltpu.VMEM((COLS, ELEM_LANES), BF16),
        pltpu.VMEM((COLS, 4 * LANES), F32),
        pltpu.VMEM((18 * COLS, BASE), BF16),
        pltpu.VMEM((18 * COLS, BASE), BF16),
        pltpu.VMEM((18 * COLS, BASE), F32),
        pltpu.SemaphoreType.DMA((SWEEPS,)),
        pltpu.SemaphoreType.DMA((SWEEPS,)),
        pltpu.SemaphoreType.DMA((SWEEPS,)),
        pltpu.SemaphoreType.DMA((SWEEPS,)),
        pltpu.SemaphoreType.DMA,
        pltpu.SemaphoreType.DMA,
    ]
    return pl.pallas_call(
        kernel,
        out_shape=(pltpu.VMEM((1, COLS, ROWS), F32), pltpu.VMEM((1, COLS, ROWS), F32)),
        in_specs=specs,
        out_specs=(vmem, vmem),
        scratch_shapes=scratch,
        compiler_params=pltpu.CompilerParams(
            collective_id=0, has_side_effects=True, vmem_limit_bytes=56 * 1024 * 1024
        ),
    )(*args)


def solution(mesh):
    placed = (
        P("zone", None, "dom"),
        P("zone", None, "dom"),
        P("zone", "dom", None, None),
        P("zone", "dom", None),
        P("dom"),
        P("dom"),
        P(None, None, "dom"),
        P(None, None, "dom"),
        P(None, None, "dom"),
        P(None, None, "dom"),
        P(None, "dom"),
        P(None, None, "dom"),
        P("dom"),
        P("dom"),
        P("dom"),
        P(None, "dom"),
        P(None, "dom"),
        P(None, "dom"),
        P(None, "dom"),
        P("dom"),
        P("dom", None, None),
        P("dom", None),
    )
    return jax.shard_map(
        on_device,
        mesh=mesh,
        in_specs=placed,
        out_specs=(P("zone", None, "dom"), P("zone", None, "dom")),
        check_vma=False,
    )
```
